32 devices in a mesh: groups: 2 (over x), wide: 8 (over z, y), narrow: 2 (over core).
Axes of the slice: x: 2, y: 2, z: 4, core: 2. Of those that a mesh axis runs over, the one named last changes fastest.
Arguments:
- tokens: bfloat16 [32, 16384], P(('groups', 'wide'), 'narrow'), parts along dimension 0, may hold values from -48 to 48
- lengths: int32 [8], P('groups'), parts along dimension 0, may hold values from 1 to 8, 16 in all
- w_query: bfloat16 [16384, 16384], P('narrow', 'wide'), may hold values from -0.046875 to 0.046875
- w_keyval: bfloat16 [16384, 2048], P('narrow', 'wide'), may hold values from -0.046875 to 0.046875
- w_out: bfloat16 [16384, 16384], P('wide', 'narrow'), may hold values from -0.046875 to 0.046875
Outputs:
- mixed: bfloat16 [32, 16384], P(('groups', 'wide'), 'narrow'), parts along dimension 0
The draws below stay inside these ranges and needn't reach their ends.
There are 2 independent parts, one for each index of `groups`. The reference program is written for one: setup_inputs(seed, part) draws one part's arguments, and reference() takes and returns one part's arrays. A program takes and returns all parts, laid end to end along the dimension named above; an argument that names none is the same for every part. Nothing has to cross between parts.
Inputs may be any that keep to these rules, and one draw needn't show every extreme that they name: The lengths sum to 16; prompt s occupies the rows after the first s lengths.
All inputs are finite; a program needn't handle non-finite values.
Results may differ from the reference program's by a relative error of at most 0.0076.
Values may be sent and summed in bfloat16 or wider, within the bound.
No kernel may reach another device: no remote copies, remote signals or barrier semaphores. Data moves between devices by JAX's collectives and lax.ppermute only.
A program may use at most 192 MiB of HBM per device.

```python
import math
import jax
import jax.numpy as jnp
import numpy as np
from jax import lax

D = 16384
HEADS = 128
KV_HEADS = 8
HEAD_DIM = 128
SEQS = 4
TOKENS = 16
MOST = 8


def draw_tokens(key, part):
    key = jax.random.fold_in(key, 11)
    base = jax.random.normal(key, (TOKENS, D), jnp.float32)
    values = jnp.clip(base, -6.0, 6.0)
    return values.astype(jnp.bfloat16)


def block_levels(rng, extent, pieces, low, top_value):
    level, own = 1.0, jax.random.fold_in(rng, 6)
    for position, shards_of in pieces:
        steps = jnp.exp(jax.random.uniform(jax.random.fold_in(own, position), (shards_of,), jnp.float32, low / len(pieces), top_value / len(pieces)))
        level = level * jnp.repeat(steps, extent[position] // shards_of).reshape([-1 if axis == position else 1 for axis in range(len(extent))])
    return level


def split_up(number_of, total, reach, skew):
    loads = [(1 << 20) // math.isqrt(standing ** skew) + 1 for standing in range(2, number_of + 1)]
    surplus, counts = total - reach - (number_of - 1), [1] * (number_of - 1)
    while surplus > 0:
        free = [i for i in range(number_of - 1) if counts[i] < reach]
        whole, left = sum([loads[i] for i in free]), surplus
        for i in free:
            addition = min(reach - counts[i], max(1, left * loads[i] // whole), surplus)
            counts[i] = counts[i] + addition
            surplus = surplus - addition
    return np.array([reach] + counts)


def ragged_sizes(stream_key, number_of, total, bound, lean):
    if number_of == 2:
        one = jax.random.randint(stream_key, (), max(1, total - bound), min(bound, total - 1) + 1)
        return jnp.stack([one, total - one])
    sizes = jnp.asarray(split_up(number_of, total, bound, lean), jnp.int32)
    twos = (number_of - 1) // 2
    source_of, taker = sizes[1:1 + 2 * twos:2], sizes[2:2 + 2 * twos:2]
    slack = jnp.minimum(source_of - 1, bound - taker)
    moved = jax.random.randint(jax.random.fold_in(stream_key, 1), (twos,), 0, 1 << 20) % (slack + 1)
    sizes = sizes.at[1:1 + 2 * twos:2].set(source_of - moved).at[2:2 + 2 * twos:2].set(taker + moved)
    return sizes[jax.random.permutation(jax.random.fold_in(stream_key, 2), number_of)]


def scatter_about(rng, dims, scale, most, split=(), kind=jnp.bfloat16):
    loudness = block_levels(rng, dims, split, -0.22, 0.18) if split else 1.0
    array = jax.random.normal(rng, dims, jnp.float32) * scale * loudness
    return jnp.minimum(jnp.maximum(array, -most), most).astype(kind)


def setup_inputs(seed: int = 0, part: int = 0) -> dict:
    arg_keys = jax.random.split(jax.random.key(seed), 6)
    part_keys = jax.random.split(jax.random.fold_in(arg_keys[5], part), 6)
    tokens = draw_tokens(jax.random.fold_in(jax.random.fold_in(arg_keys[5], part), 71), part)
    lengths = ragged_sizes(part_keys[1], SEQS, TOKENS, MOST, 2).astype(jnp.int32)
    w_query = scatter_about(arg_keys[2], (D, HEADS * HEAD_DIM), D ** -0.5, 0.046875, ((0, 2), (1, 8)))
    w_keyval = scatter_about(arg_keys[3], (D, 2 * KV_HEADS * HEAD_DIM), D ** -0.5, 0.046875, ((0, 2), (1, 8)))
    w_out = scatter_about(arg_keys[4], (HEADS * HEAD_DIM, D), (HEADS * HEAD_DIM) ** -0.5, 0.046875, ((0, 8), (1, 2)))
    return {"tokens": tokens, "lengths": lengths, "w_query": w_query, "w_keyval": w_keyval, "w_out": w_out}


theta_base = 500000.0

def positions(lengths, total):
    index = jnp.arange(total, dtype=jnp.int32)
    ends = jnp.cumsum(lengths).astype(jnp.int32)
    starts = (ends - lengths).astype(jnp.int32)
    member = (index[:, None] >= ends[None, :]).astype(jnp.int32)
    segment = lax.optimization_barrier(jnp.sum(member, axis=1)).astype(jnp.int32)
    onehot = (segment[:, None] == jnp.arange(lengths.shape[0], dtype=jnp.int32)[None, :]).astype(jnp.int32)
    offset = (index - lax.optimization_barrier(jnp.sum(onehot * starts[None, :], axis=1))).astype(jnp.int32)
    return (segment, offset)

def rotate(values, offset):
    half = values.shape[-1] // 2
    freq = theta_base ** (-(jnp.arange(half, dtype=jnp.float32) * 2.0) / values.shape[-1])
    angle = offset.astype(jnp.float32)[:, None] * freq[None, :]
    cosine = jnp.cos(angle)[:, None, :]
    sine = jnp.sin(angle)[:, None, :]
    first = values[..., :half]
    second = values[..., half:]
    return jnp.concatenate([first * cosine - second * sine, second * cosine + first * sine], axis=-1)

def attend(query, keys, values, segment):
    total = query.shape[0]
    scores = jnp.einsum('qhd,khd->hqk', query.astype(jnp.float32), keys.astype(jnp.float32)) / jnp.sqrt(jnp.float32(query.shape[-1]))
    index = jnp.arange(total, dtype=jnp.int32)
    allowed = (segment[:, None] == segment[None, :]) & (index[None, :] <= index[:, None])
    scores = jnp.where(allowed[None], scores, jnp.float32(-1e+30))
    top = lax.optimization_barrier(jnp.max(scores, axis=-1, keepdims=True))
    weights = jnp.exp(scores - top)
    probs = (weights / lax.optimization_barrier(jnp.sum(weights, axis=-1, keepdims=True))).astype(jnp.bfloat16)
    return jnp.einsum('hqk,khd->qhd', probs.astype(jnp.float32), values.astype(jnp.float32)).astype(jnp.bfloat16)

def reference(tokens, lengths, w_query, w_keyval, w_out):
    total = tokens.shape[0]
    query = jnp.dot(tokens, w_query, preferred_element_type=jnp.float32)
    keyval = jnp.dot(tokens, w_keyval, preferred_element_type=jnp.float32).astype(jnp.bfloat16)
    segment, offset = positions(lengths, total)
    kv_width = KV_HEADS * HEAD_DIM
    keys = rotate(keyval[:, :kv_width].astype(jnp.float32).reshape(total, KV_HEADS, HEAD_DIM), offset).astype(jnp.bfloat16)
    values = keyval[:, kv_width:].reshape(total, KV_HEADS, HEAD_DIM)
    kv_ids = jnp.arange(HEADS, dtype=jnp.int32) // (HEADS // KV_HEADS)
    keys_sel = jnp.take(keys, kv_ids, axis=1)
    values_sel = jnp.take(values, kv_ids, axis=1)
    query_rot = rotate(query.reshape(total, HEADS, HEAD_DIM), offset).astype(jnp.bfloat16)
    attended = attend(query_rot, keys_sel, values_sel, segment).reshape(total, HEADS * HEAD_DIM)
    return jnp.dot(attended, w_out, preferred_element_type=jnp.float32).astype(jnp.bfloat16)
```

```python
import functools
import math

import jax
import jax.numpy as jnp
import numpy as np
from jax import lax
from jax.experimental import pallas as pl
from jax.experimental.pallas import tpu as pltpu
from jax.sharding import PartitionSpec as P

HEADS = 128
KV_HEADS = 8
HEAD_DIM = 128
theta_base = 500000.0
F32 = jnp.float32
BF16 = jnp.bfloat16
MIB = 1 << 20


def vspec():
    return pl.BlockSpec(memory_space=pltpu.VMEM)


def aspec():
    return pl.BlockSpec(memory_space=pltpu.HBM)


def near(x):
    return pltpu.with_memory_space_constraint(x, pltpu.VMEM)


def call(kernel, name, ins, outs, scratch=(), limit=4, far=0, cost=0, smem=0, after=()):
    if after:
        inner, skip = kernel, len(after)
        kernel = lambda *refs: inner(*refs[skip:])
        ins = [*[near(x) for x in after], *ins]
    if far:
        ins = [*ins[:-far], *[pltpu.with_memory_space_constraint(x, pltpu.HBM) for x in ins[-far:]]]
    specs = [pl.BlockSpec(memory_space=pltpu.SMEM)] * smem
    specs += [vspec()] * (len(ins) - smem - far) + [aspec()] * far
    return pl.pallas_call(
        kernel,
        out_shape=tuple(outs),
        in_specs=specs,
        out_specs=(vspec(),) * len(outs),
        scratch_shapes=list(scratch),
        compiler_params=pltpu.CompilerParams(vmem_limit_bytes=limit * MIB),
        cost_estimate=pl.CostEstimate(flops=0, bytes_accessed=cost, transcendentals=0),
        name=name,
    )(*ins)


def fetched(w, lo, hi):
    return pltpu.VMEM((w.shape[0], hi - lo), BF16)


def fetches(sources, targets, spans, sems):
    return [
        pltpu.make_async_copy(src.at[:, pl.ds(lo, hi - lo)], dst, sems.at[i])
        for i, (src, dst, (lo, hi)) in enumerate(zip(sources, targets, spans))
    ]


def ahead_kernel(*refs, spans):
    n = len(spans)
    copies = fetches(refs[:n], refs[n : 2 * n], spans, refs[-1])
    for copy in copies:
        copy.start()
    for copy in copies:
        copy.wait()


def ahead(name, sources, spans, after=()):
    nbytes = sum(w.shape[0] * (hi - lo) * 2 for w, (lo, hi) in zip(sources, spans))
    return call(
        functools.partial(ahead_kernel, spans=spans),
        name,
        sources,
        [fetched(w, lo, hi) for w, (lo, hi) in zip(sources, spans)],
        [pltpu.SemaphoreType.DMA((len(spans),))],
        limit=1,
        far=len(sources),
        cost=nbytes,
        after=after,
    )


def join_kernel(a_ref, b_ref, o_ref):
    n = a_ref.shape[0]
    o_ref[:n] = a_ref[...]
    o_ref[n:] = b_ref[...]


def keyval_kernel(a_ref, b_ref, w_ref, *refs, order, spans):
    n = len(spans)
    sources, (x_out, kv_out), targets = refs[:n], refs[n : n + 2], refs[n + 2 : 2 * n + 2]
    x32, sems = refs[2 * n + 2 :]
    copies = fetches(sources, targets, spans, sems)
    for copy in copies:
        copy.start()
    count, rows = a_ref.shape[:2]
    for i in range(count):
        for base, ref in ((order[i], a_ref), (order[count + i], b_ref)):
            x32[rows * base : rows * (base + 1), :] = ref[i].astype(F32)
    x_out[...] = x32[...].astype(BF16)
    kv_out[...] = jnp.dot(x_out[...], w_ref[...], preferred_element_type=F32)
    for copy in copies:
        copy.wait()


def query_kernel(x_ref, *refs, parts, spans):
    n = len(spans)
    w_refs, sources, q_out, targets = refs[:parts], refs[parts : parts + n], refs[parts + n], refs[parts + n + 1 : -1]
    copies = fetches(sources, targets, spans, refs[-1])
    for copy in copies:
        copy.start()
    at = 0
    for w_ref in w_refs:
        width = w_ref.shape[1]
        step = math.gcd(width, 512)

        @pl.loop(0, width // step)
        def _(j):
            part = jnp.dot(x_ref[...], w_ref[:, pl.ds(pl.multiple_of(j * step, step), step)], preferred_element_type=F32)
            q_out[:, pl.ds(pl.multiple_of(at + j * step, step), step)] = part

        at += width
    for copy in copies:
        copy.wait()


def pair_kernel(mine_ref, other_ref, one_ref, two_ref, *, width, rows):
    me = lax.axis_index("wide")
    total = (mine_ref[...] + other_ref[...]).astype(BF16)
    row = lax.broadcasted_iota(jnp.int32, (total.shape[0],) * 2, 0)
    col = lax.broadcasted_iota(jnp.int32, (total.shape[0],) * 2, 1)
    order = (col == rows * jnp.bitwise_xor(row // rows, me) + lax.rem(row, rows)).astype(F32).astype(BF16)
    total = jnp.dot(order, total, preferred_element_type=F32)
    left, right = total[:, :width], total[:, width:]
    low = me < lax.axis_size("wide") // 2
    one_ref[...] = jnp.where(low, left, right).astype(BF16)
    two_ref[...] = jnp.where(low, right, left).astype(BF16)


def positions(token, len_ref):
    end = jnp.int32(0)
    segment = jnp.zeros_like(token)
    start = jnp.zeros_like(token)
    for i in range(len_ref.shape[0]):
        end = end + len_ref[i]
        past = token >= end
        segment = segment + past.astype(jnp.int32)
        start = start + jnp.where(past, len_ref[i], 0)
    return segment, token - start


def attend_kernel(len_ref, freq_ref, one_ref, two_ref, *refs, parts, rows, spans):
    n = len(spans)
    mine_refs, other_refs, refs = refs[:parts], refs[parts : 2 * parts], refs[2 * parts :]
    sources, att, targets, sems = refs[:n], refs[n], refs[n + 1 : -1], refs[-1]
    copies = fetches(sources, targets, spans, sems)
    for copy in copies:
        copy.start()
    me = lax.axis_index("wide")
    total, dim = one_ref.shape
    odd = lax.rem(me, 2) == 1
    one, two = one_ref[...].astype(F32), two_ref[...].astype(F32)
    keys = jnp.where(odd, two, one)
    values = jnp.where(odd, one, two).astype(BF16)
    freq = freq_ref[...]

    def owner(row):
        return rows * jnp.bitwise_xor(row // rows, me) + lax.rem(row, rows)

    def tables(token):
        angle = positions(token, len_ref)[1].astype(F32) * freq
        lane = lax.broadcasted_iota(jnp.int32, angle.shape, 1)
        sine = jnp.sin(angle)
        return jnp.cos(angle), jnp.where(lane < dim // 2, -sine, sine)

    def rotate(u, cosine, sine):
        return u * cosine + pltpu.roll(u, dim // 2, 1) * sine

    row = lax.broadcasted_iota(jnp.int32, (total, dim), 0)
    keys_rot = rotate(keys, *tables(row)).astype(BF16)
    cosine, sine = tables(owner(row))
    turned = []
    for mine_ref, other_ref in zip(mine_refs, other_refs):
        query = mine_ref[...] + other_ref[...]
        for h in range(query.shape[1] // dim):
            turned.append(rotate(query[:, dim * h : dim * (h + 1)], cosine, sine).astype(BF16))
    stack = jnp.concatenate(turned, axis=0)
    scores = lax.dot_general(stack, keys_rot, (((1,), (1,)), ((), ())), preferred_element_type=F32)
    scores = scores / F32(math.sqrt(dim))
    qtok = owner(lax.rem(lax.broadcasted_iota(jnp.int32, scores.shape, 0), total))
    ktok = lax.broadcasted_iota(jnp.int32, scores.shape, 1)
    allowed = (positions(qtok, len_ref)[0] == positions(ktok, len_ref)[0]) & (ktok <= qtok)
    scores = jnp.where(allowed, scores, F32(-1e30))
    weights = jnp.exp(scores - jnp.max(scores, axis=1, keepdims=True))
    probs = (weights / jnp.sum(weights, axis=1, keepdims=True)).astype(BF16)
    mixed = jnp.dot(probs, values, preferred_element_type=F32).astype(BF16)
    for h in range(len(turned)):
        att[:, dim * h : dim * (h + 1)] = mixed[total * h : total * (h + 1), :]
    for copy in copies:
        copy.wait()


def output_kernel(att_ref, *refs, near_parts, lo, hi, pieces, spans):
    n = len(spans)
    w_refs, refs = refs[:near_parts], refs[near_parts:]
    sources, refs = refs[:n], refs[n:]
    keep_ref, send_ref, targets = refs[0], refs[1], refs[2 : 2 + n]
    acc, sems = refs[2 + n :]
    copies = fetches(sources, targets, spans, sems)
    for copy in copies:
        copy.start()
    at = 0
    for k, w_ref in enumerate(w_refs):
        width = w_ref.shape[1]
        step = math.gcd(width, 512)

        @pl.loop(0, width // step)
        def _(j):
            part = jnp.dot(att_ref[...], w_ref[:, pl.ds(pl.multiple_of(j * step, step), step)], preferred_element_type=F32)
            acc[:, pl.ds(pl.multiple_of(at + j * step, step), step)] = part

        at += width
    rows = acc.shape[0] // pieces
    for s in range(0, pieces, 2):
        keep_ref[s // 2] = acc[rows * s : rows * (s + 1), :]
        send_ref[s // 2] = acc[rows * (s + 1) : rows * (s + 2), :].astype(BF16)
    for copy in copies:
        copy.wait()


def near_sum_kernel(keep_ref, got_ref, own_ref, *outs):
    for k in range(keep_ref.shape[0]):
        part = keep_ref[k] + got_ref[k].astype(F32)
        if k == 0:
            own_ref[...] = part
        else:
            outs[k - 1][...] = part.astype(BF16)


def total_kernel(*refs, parts, count):
    out = refs[-1]
    at = 0
    for p in range(parts):
        mine = refs[p * count]
        total = mine[...]
        for r in refs[p * count + 1 : (p + 1) * count]:
            total = total + r[...].astype(F32)
        out[:, at : at + mine.shape[1]] = total.astype(BF16)
        at += mine.shape[1]


def swap(x, axis, size, bit):
    return lax.ppermute(x, axis, [(i, i ^ bit) for i in range(size)])


def shaped(*shape, dtype=F32):
    return jax.ShapeDtypeStruct(shape, dtype)


def plain_positions(lengths, total):
    index = jnp.arange(total, dtype=jnp.int32)
    ends = jnp.cumsum(lengths)
    past = index[:, None] >= ends[None, :]
    segment = jnp.sum(past.astype(jnp.int32), axis=1)
    offset = index - jnp.sum(jnp.where(past, lengths[None, :], 0), axis=1)
    return segment, offset


def plain_rotate(values, offset):
    half = values.shape[-1] // 2
    freq = theta_base ** (-(jnp.arange(half, dtype=F32) * 2.0) / values.shape[-1])
    angle = offset.astype(F32)[:, None] * freq[None, :]
    cosine = jnp.cos(angle)[:, None, :]
    sine = jnp.sin(angle)[:, None, :]
    first, second = values[..., :half], values[..., half:]
    return jnp.concatenate([first * cosine - second * sine, second * cosine + first * sine], axis=-1)


def plain_attend(query, keys, values, segment):
    total = query.shape[0]
    scores = jnp.einsum("qhd,khd->hqk", query, keys, preferred_element_type=F32) / jnp.sqrt(F32(query.shape[-1]))
    index = jnp.arange(total, dtype=jnp.int32)
    allowed = (segment[:, None] == segment[None, :]) & (index[None, :] <= index[:, None])
    scores = jnp.where(allowed[None], scores, F32(-1e30))
    weights = jnp.exp(scores - jnp.max(scores, axis=-1, keepdims=True))
    probs = (weights / jnp.sum(weights, axis=-1, keepdims=True)).astype(BF16)
    return jnp.einsum("hqk,khd->qhd", probs, values, preferred_element_type=F32).astype(BF16)


def plain(tokens, lengths, w_query, w_keyval, w_out):
    q_cols = w_query.shape[1]
    heads = q_cols // HEAD_DIM
    piece = lax.all_gather(tokens, "wide", axis=0, tiled=True)
    query_part = jnp.dot(piece, w_query, preferred_element_type=F32)
    keyval_part = jnp.dot(piece, w_keyval, preferred_element_type=F32)
    total = piece.shape[0]
    query = lax.psum(query_part, "narrow")
    summed = lax.psum(keyval_part, "narrow").astype(BF16)
    keyval = lax.all_gather(summed, "wide", axis=1, tiled=True)
    segment, offset = plain_positions(lengths, total)
    kv_width = KV_HEADS * HEAD_DIM
    keys = plain_rotate(keyval[:, :kv_width].astype(F32).reshape(total, KV_HEADS, HEAD_DIM), offset).astype(BF16)
    values = keyval[:, kv_width:].reshape(total, KV_HEADS, HEAD_DIM)
    head_ids = lax.axis_index("wide") * heads + jnp.arange(heads, dtype=jnp.int32)
    kv_ids = head_ids // (HEADS // KV_HEADS)
    query_rot = plain_rotate(query.reshape(total, -1, HEAD_DIM), offset).astype(BF16)
    attended = plain_attend(query_rot, jnp.take(keys, kv_ids, axis=1), jnp.take(values, kv_ids, axis=1), segment)
    mixed = lax.psum_scatter(
        jnp.dot(attended.reshape(total, -1), w_out, preferred_element_type=F32), "wide", scatter_dimension=0, tiled=True
    )
    return mixed.astype(BF16)


def local(tokens, lengths, w_query, w_keyval, w_out):
    wide = lax.axis_size("wide")
    rows, depth = tokens.shape
    total = rows * wide
    kv_cols, q_cols, out_cols = w_keyval.shape[1], w_query.shape[1], w_out.shape[1]
    inner = w_out.shape[0]
    bits = [1 << b for b in reversed(range(wide.bit_length() - 1))]
    cuts = [0, q_cols // 8, 3 * q_cols // 8, 7 * q_cols // 8]
    x = tokens[None]
    order = [0]
    w_near = []
    kv_near = None
    for i, bit in enumerate(bits):
        other = swap(x, "wide", wide, bit)
        if i == 0:
            kv_near, w0 = ahead("ahead%d" % i, [w_keyval, w_query], [(0, kv_cols), (cuts[0], cuts[1])])
        else:
            (w0,) = ahead("ahead%d" % i, [w_query], [(cuts[i], cuts[i + 1])], after=[x])
        w_near.append(w0)
        order = order + [s ^ bit for s in order]
        if i < len(bits) - 1:
            (x,) = call(join_kernel, "join%d" % i, [x, other], [shaped(2 * x.shape[0], rows, depth, dtype=BF16)], limit=2, after=[w0])
    x, kv, w3 = call(
        functools.partial(keyval_kernel, order=order, spans=[(cuts[3], q_cols)]),
        "keyval",
        [x, other, near(kv_near), w_query],
        [shaped(total, depth, dtype=BF16), shaped(total, kv_cols), fetched(w_query, cuts[3], q_cols)],
        [pltpu.VMEM((total, depth), F32), pltpu.SemaphoreType.DMA((1,))],
        limit=4,
        far=1,
        after=[w_near[-1]],
    )
    w_near.append(w3)
    kv_other = swap(kv, "narrow", 2, 1)
    o_cuts = [0, out_cols // 8, 3 * out_cols // 8, out_cols // 2, out_cols * 5 // 8, out_cols]

    def query(name, weights, span, after=()):
        return call(
            functools.partial(query_kernel, parts=len(weights), spans=[span]),
            name,
            [x, *[near(w) for w in weights], w_out],
            [shaped(total, sum(w.shape[1] for w in weights)), fetched(w_out, *span)],
            [pltpu.SemaphoreType.DMA((1,))],
            limit=2,
            far=1,
            cost=sum(w.size * 2 for w in weights),
            after=after,
        )

    q0, o0 = query("query0", w_near[:2], (o_cuts[0], o_cuts[1]))
    one, two = call(
        functools.partial(pair_kernel, width=HEAD_DIM, rows=rows),
        "pair",
        [kv, kv_other],
        [shaped(total, HEAD_DIM, dtype=BF16)] * 2,
        limit=1,
        after=[o0],
    )
    half = wide // 2
    first = [(s, 2 * s) if s < half else (s, 2 * (s - half) + 1) for s in range(wide)]
    second = [(s, 2 * s + 1) if s < half else (s, 2 * (s - half)) for s in range(wide)]
    sent = one
    one = lax.ppermute(one, "wide", first)
    two = lax.ppermute(two, "wide", second)
    q0_other = swap(q0, "narrow", 2, 1)
    q1, o1 = query("query1", w_near[2:], (o_cuts[1], o_cuts[2]), after=[sent])
    q1_other = swap(q1, "narrow", 2, 1)
    (o2,) = ahead("ahead_out", [w_out], [(o_cuts[2], o_cuts[3])], after=[q1])
    freq = theta_base ** (-(np.arange(HEAD_DIM) % (HEAD_DIM // 2)) * 2.0 / HEAD_DIM)
    freq = jnp.asarray(freq[None, :], F32)
    att, o3 = call(
        functools.partial(attend_kernel, parts=2, rows=rows, spans=[(o_cuts[3], o_cuts[4])]),
        "attend",
        [lengths, freq, one, two, q0, q1, q0_other, q1_other, w_out],
        [shaped(total, q_cols, dtype=BF16), fetched(w_out, o_cuts[3], o_cuts[4])],
        [pltpu.SemaphoreType.DMA((1,))],
        limit=4,
        far=1,
        smem=1,
    )

    def output(name, weights, span):
        width = sum(w.shape[1] for w in weights)
        return call(
            functools.partial(output_kernel, near_parts=len(weights), lo=0, hi=0, pieces=wide, spans=[span] if span else []),
            name,
            [att, *[near(w) for w in weights], *([w_out] if span else [])],
            [shaped(wide // 2, rows, width), shaped(wide // 2, rows, width, dtype=BF16)]
            + ([fetched(w_out, *span)] if span else []),
            [pltpu.VMEM((total, width), F32), pltpu.SemaphoreType.DMA((1,))],
            limit=4,
            far=1 if span else 0,
            cost=sum(w.size * 2 for w in weights),
        )

    keep0, send0, o4 = output("output0", [o0, o1, o2, o3], (o_cuts[4], o_cuts[5]))
    got0 = swap(send0, "wide", wide, 1)
    keep1, send1 = output("output1", [o4], None)
    got1 = swap(send1, "wide", wide, 1)

    def finish(name, keep, got):
        count, _, width = keep.shape
        mine, *others = call(
            near_sum_kernel,
            name,
            [keep, got],
            [shaped(rows, width)] + [shaped(rows, width, dtype=BF16)] * (count - 1),
            limit=1,
        )
        back = {k: swap(others[k - 1], "wide", wide, 2 * k) for k in reversed(range(1, count))}
        return [mine] + [back[k] for k in range(1, count)]

    parts = finish("sum0", keep0, got0) + finish("sum1", keep1, got1)
    return call(
        functools.partial(total_kernel, parts=2, count=wide // 2),
        "total",
        parts,
        [shaped(rows, out_cols, dtype=BF16)],
        limit=1,
    )[0]


def solution(mesh):
    in_specs = (
        P(("groups", "wide"), "narrow"),
        P("groups"),
        P("narrow", "wide"),
        P("narrow", "wide"),
        P("wide", "narrow"),
    )
    out_specs = P(("groups", "wide"), "narrow")
    body = local if mesh.shape["wide"] == KV_HEADS and mesh.shape["narrow"] == 2 else plain
    return jax.shard_map(body, mesh=mesh, in_specs=in_specs, out_specs=out_specs, check_vma=False)
```

```python
import functools
import math

import jax
import jax.numpy as jnp
from jax import lax
from jax.experimental import pallas as pl
from jax.experimental.pallas import tpu as pltpu
from jax.sharding import PartitionSpec as P

HEADS = 128
KV_HEADS = 8
HEAD_DIM = 128
theta_base = 500000.0
F32 = jnp.float32
BF16 = jnp.bfloat16
MIB = 1 << 20
CUTS = (0, 6, 9, 9, 10, 22, 24, 24, 32)
QSTEP = 4
QOUT = pltpu.VMEM
LIM = 3
HINT = 0
JH = (0, 0)
KH = 0


def vspec():
    return pl.BlockSpec(memory_space=pltpu.VMEM)


def aspec():
    return pl.BlockSpec(memory_space=pltpu.HBM)


def near(x):
    return pltpu.with_memory_space_constraint(x, pltpu.VMEM)


def call(kernel, name, ins, outs, scratch=(), limit=4, far=0, hint=0, smem=0, after=(), behind=()):
    if after:
        inner, skip = kernel, len(after)
        kernel = lambda *refs: inner(*refs[skip:])
        ins = [*[near(x) for x in after], *ins]
    if behind:
        whole, drop, keep = kernel, len(behind), len(ins) + len(after)
        kernel = lambda *refs: whole(*refs[:keep], *refs[keep + drop :])
        ins, far = [*ins, *behind], far + drop
    if far:
        ins = [*ins[:-far], *[pltpu.with_memory_space_constraint(x, pltpu.HBM) for x in ins[-far:]]]
    specs = [pl.BlockSpec(memory_space=pltpu.SMEM)] * smem
    specs += [vspec()] * (len(ins) - smem - far) + [aspec()] * far
    return pl.pallas_call(
        kernel,
        out_shape=tuple(outs),
        in_specs=specs,
        out_specs=(vspec(),) * len(outs),
        scratch_shapes=list(scratch),
        compiler_params=pltpu.CompilerParams(vmem_limit_bytes=limit * MIB),
        cost_estimate=pl.CostEstimate(flops=hint, bytes_accessed=1000, transcendentals=0),
        name=name,
    )(*ins)


def fetched(w, lo, hi):
    return pltpu.VMEM((w.shape[0], hi - lo), BF16)


def fetches(sources, targets, spans, sems):
    return [
        pltpu.make_async_copy(src.at[:, pl.ds(lo, hi - lo)], dst, sems.at[i])
        for i, (src, dst, (lo, hi)) in enumerate(zip(sources, targets, spans))
    ]


def ahead_kernel(*refs, spans):
    n = len(spans)
    copies = fetches(refs[:n], refs[n : 2 * n], spans, refs[-1])
    for copy in copies:
        copy.start()
    for copy in copies:
        copy.wait()


def ahead(name, sources, spans, after=(), behind=(), hint=0):
    return call(
        functools.partial(ahead_kernel, spans=spans),
        name,
        sources,
        [fetched(w, lo, hi) for w, (lo, hi) in zip(sources, spans)],
        [pltpu.SemaphoreType.DMA((len(spans),))],
        limit=1,
        far=len(sources),
        hint=hint,
        after=after,
        behind=behind,
    )


def positions(token, len_ref):
    end = jnp.int32(0)
    segment = jnp.zeros_like(token)
    start = jnp.zeros_like(token)
    for i in range(len_ref.shape[0]):
        end = end + len_ref[i]
        past = token >= end
        segment = segment + past.astype(jnp.int32)
        start = start + jnp.where(past, len_ref[i], 0)
    return segment, token - start


def tables_kernel(*refs, rows, spans):
    n = len(spans)
    sources, (turn_ref, allow_ref), targets, (sems, len_ref, len_sem) = refs[: n + 1], refs[n + 1 : n + 3], refs[n + 3 : -3], refs[-3:]
    lengths = pltpu.make_async_copy(sources[0], len_ref, len_sem)
    lengths.start()
    copies = fetches(sources[1:], targets, spans, sems)
    for copy in copies:
        copy.start()
    me = lax.axis_index("wide")
    total, dim = turn_ref.shape[1:]

    def owner(row, base):
        return rows * jnp.bitwise_xor(row // rows, base) + lax.rem(row, rows)

    shape = (total, dim)
    power = lax.rem(lax.broadcasted_iota(jnp.int32, shape, 1), dim // 2).astype(F32)
    freq = jnp.exp(power * F32(-2.0 * math.log(theta_base) / dim))
    lengths.wait()
    row = lax.broadcasted_iota(jnp.int32, shape, 0)
    lane = lax.broadcasted_iota(jnp.int32, shape, 1)
    for i, base in enumerate((me, me // 2)):
        angle = positions(owner(row, base), len_ref)[1].astype(F32) * freq
        sine = jnp.sin(angle)
        turn_ref[2 * i] = jnp.cos(angle)
        turn_ref[2 * i + 1] = jnp.where(lane < dim // 2, -sine, sine)
    shape = allow_ref.shape
    query = owner(lax.rem(lax.broadcasted_iota(jnp.int32, shape, 0), total), me)
    key = owner(lax.broadcasted_iota(jnp.int32, shape, 1), me // 2)
    same = positions(query, len_ref)[0] == positions(key, len_ref)[0]
    allow_ref[...] = jnp.where(same & (key <= query), 1.0, 0.0).astype(F32)
    for copy in copies:
        copy.wait()


def join_kernel(a_ref, b_ref, o_ref):
    n = a_ref.shape[0]
    o_ref[:n] = a_ref[...]
    o_ref[n:] = b_ref[...]


def keyval_kernel(a_ref, b_ref, w_ref, *refs, order, spans):
    n = len(spans)
    sources, (x_out, keep_ref, give_ref), targets = refs[:n], refs[n : n + 3], refs[n + 3 : 2 * n + 3]
    x32, sems = refs[2 * n + 3 :]
    copies = fetches(sources, targets, spans, sems)
    for copy in copies:
        copy.start()
    count, rows = a_ref.shape[:2]
    for i in range(count):
        for base, ref in ((order[i], a_ref), (order[count + i], b_ref)):
            x32[rows * base : rows * (base + 1), :] = ref[i].astype(F32)
    x_out[...] = x32[...].astype(BF16)
    part = jnp.dot(x_out[...], w_ref[...], preferred_element_type=F32)
    width = keep_ref.shape[1]
    left, right = part[:, :width], part[:, width:]
    low = lax.axis_index("narrow") == 0
    keep_ref[...] = jnp.where(low, left, right)
    give_ref[...] = jnp.where(low, right, left)
    for copy in copies:
        copy.wait()


def pair_kernel(mine_ref, other_ref, out_ref):
    out_ref[...] = (mine_ref[...] + other_ref[...]).astype(BF16)


def multiply(x_ref, w_ref, out, at, lo=0, hi=None):
    width = (w_ref.shape[1] if hi is None else hi) - lo
    step = math.gcd(math.gcd(width, 512), lo)

    @pl.loop(0, width // step)
    def _(j):
        cols = pl.ds(pl.multiple_of(lo + j * step, step), step)
        part = jnp.dot(x_ref[...], w_ref[:, cols], preferred_element_type=F32)
        out[:, pl.ds(pl.multiple_of(at + j * step, step), step)] = part


def query_kernel(x_ref, w_ref, head_ref, *refs, spans):
    n = len(spans)
    sources, q_out, targets, sems = refs[:n], refs[n], refs[n + 1 : -1], refs[-1]
    copies = fetches(sources, targets, spans, sems)
    for copy in copies:
        copy.start()
    width = head_ref.shape[1]
    q_out[:, :width] = head_ref[...].astype(F32)
    multiply(x_ref, w_ref, q_out, width)
    for copy in copies:
        copy.wait()


def attend(mine_ref, other_ref, turn_ref, allow_ref, att):
    total, dim = turn_ref.shape[1:]
    low = lax.axis_index("narrow") == 0
    mine, other = mine_ref[:, :dim], other_ref[:, :dim]
    keys, values = jnp.where(low, mine, other), jnp.where(low, other, mine)
    summed = mine_ref[:, dim:] + other_ref[:, dim:]
    values = jnp.concatenate([values[total // 2 :], values[: total // 2]], axis=0).astype(BF16)

    def rotate(u, i):
        return (u * turn_ref[i] + pltpu.roll(u, dim // 2, 1) * turn_ref[i + 1]).astype(BF16)

    keys = rotate(keys, 2)
    heads = summed.shape[1] // dim
    stack = jnp.concatenate([rotate(summed[:, dim * h : dim * (h + 1)], 0) for h in range(heads)], axis=0)
    scores = lax.dot_general(stack, keys, (((1,), (1,)), ((), ())), preferred_element_type=F32)
    scores = scores / F32(math.sqrt(dim))
    scores = jnp.where(allow_ref[...] > 0, scores, F32(-1e30))
    weights = jnp.exp(scores - jnp.max(scores, axis=1, keepdims=True))
    probs = (weights / jnp.sum(weights, axis=1, keepdims=True)).astype(BF16)
    mixed = jnp.dot(probs, values, preferred_element_type=F32).astype(BF16)
    for h in range(heads):
        att[:, dim * h : dim * (h + 1)] = mixed[total * h : total * (h + 1), :]


def part_out(acc, keep_ref, send_ref):
    pieces = 2 * keep_ref.shape[0]
    rows = acc.shape[0] // pieces
    for s in range(0, pieces, 2):
        keep_ref[s // 2] = acc[rows * s : rows * (s + 1), :]
        send_ref[s // 2] = acc[rows * (s + 1) : rows * (s + 2), :].astype(BF16)


def output_kernel(*refs, first, parts, own, spans):
    n = len(spans)
    if first:
        head, refs = refs[:4], refs[4:]
    else:
        att, refs = refs[0], refs[1:]
    w_refs, refs = refs[:parts], refs[parts:]
    w_far = None
    if n or own:
        w_far, refs = refs[0], refs[1:]
    if first:
        att, refs = refs[0], refs[1:]
    keep_ref, send_ref, targets, refs = refs[0], refs[1], refs[2 : 2 + n], refs[2 + n :]
    acc, sems, mine = refs[0], refs[1], refs[2:]
    copies = fetches([w_far] * (len(own) + n), [*mine, *targets], [*own, *spans], sems)
    for copy in copies:
        copy.start()
    if first:
        attend(*head, att)
    at = 0
    for w_ref in w_refs:
        multiply(att, w_ref, acc, at)
        at += w_ref.shape[1]
    for copy, w_ref in zip(copies, mine):
        copy.wait()
        multiply(att, w_ref, acc, at)
        at += w_ref.shape[1]
    part_out(acc, keep_ref, send_ref)
    for copy in copies[len(own) :]:
        copy.wait()


def near_sum_kernel(*refs, parts):
    at = 0
    outs = refs[2 * parts :]
    for p in range(parts):
        keep_ref, got_ref = refs[2 * p : 2 * p + 2]
        width = keep_ref.shape[2]
        for k in range(keep_ref.shape[0]):
            part = keep_ref[k] + got_ref[k].astype(F32)
            outs[k][:, at : at + width] = part.astype(outs[k].dtype)
        at += width


def total_kernel(*refs):
    total = refs[0][...]
    for r in refs[1:-1]:
        total = total + r[...].astype(F32)
    refs[-1][...] = total.astype(BF16)


def swap(x, axis, size, bit):
    return lax.ppermute(x, axis, [(i, i ^ bit) for i in range(size)])


def shaped(*shape, dtype=F32):
    return jax.ShapeDtypeStruct(shape, dtype)


def plain_positions(lengths, total):
    index = jnp.arange(total, dtype=jnp.int32)
    ends = jnp.cumsum(lengths)
    past = index[:, None] >= ends[None, :]
    segment = jnp.sum(past.astype(jnp.int32), axis=1)
    offset = index - jnp.sum(jnp.where(past, lengths[None, :], 0), axis=1)
    return segment, offset


def plain_rotate(values, offset):
    half = values.shape[-1] // 2
    freq = theta_base ** (-(jnp.arange(half, dtype=F32) * 2.0) / values.shape[-1])
    angle = offset.astype(F32)[:, None] * freq[None, :]
    cosine = jnp.cos(angle)[:, None, :]
    sine = jnp.sin(angle)[:, None, :]
    first, second = values[..., :half], values[..., half:]
    return jnp.concatenate([first * cosine - second * sine, second * cosine + first * sine], axis=-1)


def plain_attend(query, keys, values, segment):
    total = query.shape[0]
    scores = jnp.einsum("qhd,khd->hqk", query, keys, preferred_element_type=F32) / jnp.sqrt(F32(query.shape[-1]))
    index = jnp.arange(total, dtype=jnp.int32)
    allowed = (segment[:, None] == segment[None, :]) & (index[None, :] <= index[:, None])
    scores = jnp.where(allowed[None], scores, F32(-1e30))
    weights = jnp.exp(scores - jnp.max(scores, axis=-1, keepdims=True))
    probs = (weights / jnp.sum(weights, axis=-1, keepdims=True)).astype(BF16)
    return jnp.einsum("hqk,khd->qhd", probs, values, preferred_element_type=F32).astype(BF16)


def plain(tokens, lengths, w_query, w_keyval, w_out):
    q_cols = w_query.shape[1]
    heads = q_cols // HEAD_DIM
    piece = lax.all_gather(tokens, "wide", axis=0, tiled=True)
    query_part = jnp.dot(piece, w_query, preferred_element_type=F32)
    keyval_part = jnp.dot(piece, w_keyval, preferred_element_type=F32)
    total = piece.shape[0]
    query = lax.psum(query_part, "narrow")
    summed = lax.psum(keyval_part, "narrow").astype(BF16)
    keyval = lax.all_gather(summed, "wide", axis=1, tiled=True)
    segment, offset = plain_positions(lengths, total)
    kv_width = KV_HEADS * HEAD_DIM
    keys = plain_rotate(keyval[:, :kv_width].astype(F32).reshape(total, KV_HEADS, HEAD_DIM), offset).astype(BF16)
    values = keyval[:, kv_width:].reshape(total, KV_HEADS, HEAD_DIM)
    head_ids = lax.axis_index("wide") * heads + jnp.arange(heads, dtype=jnp.int32)
    kv_ids = head_ids // (HEADS // KV_HEADS)
    query_rot = plain_rotate(query.reshape(total, -1, HEAD_DIM), offset).astype(BF16)
    attended = plain_attend(query_rot, jnp.take(keys, kv_ids, axis=1), jnp.take(values, kv_ids, axis=1), segment)
    mixed = lax.psum_scatter(
        jnp.dot(attended.reshape(total, -1), w_out, preferred_element_type=F32), "wide", scatter_dimension=0, tiled=True
    )
    return mixed.astype(BF16)


def local(tokens, lengths, w_query, w_keyval, w_out):
    wide = lax.axis_size("wide")
    rows, depth = tokens.shape
    total = rows * wide
    kv_cols, q_cols, out_cols = w_keyval.shape[1], w_query.shape[1], w_out.shape[1]
    heads = q_cols // HEAD_DIM

    bits = [1 << b for b in reversed(range(wide.bit_length() - 1))]
    o_cuts = [out_cols * k // 32 for k in CUTS]
    x, order, o_near = tokens[None], [0], []
    for i, bit in enumerate(bits):
        other = swap(x, "wide", wide, bit)
        w = None
        span = (o_cuts[i], o_cuts[i + 1])
        if i == 0:
            spans = [span] if span[1] > span[0] else []
            turn, allow, *pieces = call(
                functools.partial(tables_kernel, rows=rows, spans=spans),
                "tables",
                [lengths, *[w_out for _ in spans]],
                [shaped(4, total, HEAD_DIM), shaped(heads * total, total)] + [fetched(w_out, *s) for s in spans],
                [pltpu.SemaphoreType.DMA((1,)), pltpu.SMEM(lengths.shape, jnp.int32), pltpu.SemaphoreType.DMA],
                limit=2,
                far=1 + len(spans),
                hint=HINT,
            )
            o_near += pieces
            w = turn
        elif span[1] > span[0]:
            (w,) = ahead("ahead%d" % i, [w_out], [span], after=[x])
            o_near.append(w)
        order = order + [s ^ bit for s in order]
        if i < len(bits) - 1:
            (x,) = call(join_kernel, "join%d" % i, [x, other], [shaped(2 * x.shape[0], rows, depth, dtype=BF16)], limit=2, after=[] if w is None else [w], hint=JH[i])
    x, keep, give = call(
        functools.partial(keyval_kernel, order=order, spans=[]),
        "keyval",
        [x, other, near(w_keyval)],
        [shaped(total, depth, dtype=BF16)] + [shaped(total, HEAD_DIM)] * 2,
        [pltpu.VMEM((total, depth), F32), pltpu.SemaphoreType.DMA((1,))],
        limit=4,
        hint=KH,
        after=[o_near[-1]],
    )

    half = wide // 2
    given = swap(give, "narrow", 2, 1)
    (head,) = call(pair_kernel, "pair", [keep, given], [shaped(total, HEAD_DIM, dtype=BF16)], limit=1)
    routes = [(2 * s + n, 2 * ((2 * s + n) % wide) + s // half) for s in range(wide) for n in range(2)]
    sent = head
    head = lax.ppermute(head, ("wide", "narrow"), routes)
    if o_cuts[4] > o_cuts[3]:
        (w,) = ahead("ahead3", [w_out], [(o_cuts[3], o_cuts[4])], after=[sent])
        o_near.append(w)
    unit = out_cols * QSTEP // 32
    spans = [(lo, min(lo + unit, o_cuts[5])) for lo in range(o_cuts[4], o_cuts[5], unit)]
    q, *pieces = call(
        functools.partial(query_kernel, spans=spans),
        "query",
        [x, near(w_query), head] + [w_out] * len(spans),
        [QOUT((total, q_cols + HEAD_DIM), F32)] + [fetched(w_out, *span) for span in spans],
        [pltpu.SemaphoreType.DMA((len(spans),))],
        limit=2,
        far=len(spans),
        after=o_near[-1:],
    )
    o_near += pieces
    other = swap(q, "narrow", 2, 1)
    if o_cuts[6] > o_cuts[5]:
        (w,) = ahead("ahead4", [w_out], [(o_cuts[5], o_cuts[6])], after=[q])
        o_near.append(w)

    def output(name, head, weights, own, spans):
        own_cols = [hi - lo for lo, hi in own]
        width = sum(w.shape[1] for w in weights) + sum(own_cols)
        return call(
            functools.partial(output_kernel, first=len(head) > 1, parts=len(weights), own=own, spans=spans),
            name,
            [*head, *[near(w) for w in weights], *([w_out] if own or spans else [])],
            ([shaped(total, q_cols, dtype=BF16)] if len(head) > 1 else [])
            + [shaped(wide // 2, rows, width), shaped(wide // 2, rows, width, dtype=BF16)]
            + [fetched(w_out, *span) for span in spans],
            [pltpu.VMEM((total, width), F32), pltpu.SemaphoreType.DMA((max(1, len(own) + len(spans)),))]
            + [pltpu.VMEM((w_out.shape[0], cols), BF16) for cols in own_cols],
            limit=LIM,
            far=1 if own or spans else 0,
        )

    att, keep0, send0, o2 = output(
        "output0",
        [q, other, turn, allow],
        o_near,
        [span for span in [(o_cuts[6], o_cuts[7])] if span[1] > span[0]],
        [(o_cuts[7], o_cuts[8])],
    )
    got0 = swap(send0, "wide", wide, 1)
    keep1, send1 = output("output1", [att], [o2], [], [])
    got1 = swap(send1, "wide", wide, 1)
    mine, *others = call(
        functools.partial(near_sum_kernel, parts=2),
        "pairs",
        [keep0, got0, keep1, got1],
        [shaped(rows, out_cols)] + [shaped(rows, out_cols, dtype=BF16)] * (half - 1),
        limit=1,
    )
    back = {k: swap(others[k - 1], "wide", wide, 2 * k) for k in reversed(range(1, half))}
    return call(total_kernel, "total", [mine] + [back[k] for k in range(1, half)], [shaped(rows, out_cols, dtype=BF16)], limit=1)[0]


def solution(mesh):
    in_specs = (
        P(("groups", "wide"), "narrow"),
        P("groups"),
        P("narrow", "wide"),
        P("narrow", "wide"),
        P("wide", "narrow"),
    )
    out_specs = P(("groups", "wide"), "narrow")
    body = local if mesh.shape["wide"] == KV_HEADS and mesh.shape["narrow"] == 2 else plain
    return jax.shard_map(body, mesh=mesh, in_specs=in_specs, out_specs=out_specs, check_vma=False)
```

```python
import functools
import math

import jax
import jax.numpy as jnp
from jax import lax
from jax.experimental import pallas as pl
from jax.experimental.pallas import tpu as pltpu
from jax.sharding import PartitionSpec as P

HEADS = 128
KV_HEADS = 8
HEAD_DIM = 128
theta_base = 500000.0
F32 = jnp.float32
BF16 = jnp.bfloat16
MIB = 1 << 20
CUTS = (0, 6, 6, 9, 10, 22, 24, 24, 32)
QSTEP = 4
QOUT = pltpu.VMEM
LIM = 3
HINT = 0
JH = (0, 0)
KH = 0


def vspec():
    return pl.BlockSpec(memory_space=pltpu.VMEM)


def aspec():
    return pl.BlockSpec(memory_space=pltpu.HBM)


def near(x):
    return pltpu.with_memory_space_constraint(x, pltpu.VMEM)


def call(kernel, name, ins, outs, scratch=(), limit=4, far=0, hint=0, smem=0, after=(), behind=()):
    if after:
        inner, skip = kernel, len(after)
        kernel = lambda *refs: inner(*refs[skip:])
        ins = [*[near(x) for x in after], *ins]
    if behind:
        whole, drop, keep = kernel, len(behind), len(ins) + len(after)
        kernel = lambda *refs: whole(*refs[:keep], *refs[keep + drop :])
        ins, far = [*ins, *behind], far + drop
    if far:
        ins = [*ins[:-far], *[pltpu.with_memory_space_constraint(x, pltpu.HBM) for x in ins[-far:]]]
    specs = [pl.BlockSpec(memory_space=pltpu.SMEM)] * smem
    specs += [vspec()] * (len(ins) - smem - far) + [aspec()] * far
    return pl.pallas_call(
        kernel,
        out_shape=tuple(outs),
        in_specs=specs,
        out_specs=(vspec(),) * len(outs),
        scratch_shapes=list(scratch),
        compiler_params=pltpu.CompilerParams(vmem_limit_bytes=limit * MIB),
        cost_estimate=pl.CostEstimate(flops=hint, bytes_accessed=1000, transcendentals=0),
        name=name,
    )(*ins)


def fetched(w, lo, hi):
    return pltpu.VMEM((w.shape[0], hi - lo), BF16)


def fetches(sources, targets, spans, sems):
    return [
        pltpu.make_async_copy(src.at[:, pl.ds(lo, hi - lo)], dst, sems.at[i])
        for i, (src, dst, (lo, hi)) in enumerate(zip(sources, targets, spans))
    ]


def ahead_kernel(*refs, spans):
    n = len(spans)
    copies = fetches(refs[:n], refs[n : 2 * n], spans, refs[-1])
    for copy in copies:
        copy.start()
    for copy in copies:
        copy.wait()


def ahead(name, sources, spans, after=(), behind=(), hint=0):
    return call(
        functools.partial(ahead_kernel, spans=spans),
        name,
        sources,
        [fetched(w, lo, hi) for w, (lo, hi) in zip(sources, spans)],
        [pltpu.SemaphoreType.DMA((len(spans),))],
        limit=1,
        far=len(sources),
        hint=hint,
        after=after,
        behind=behind,
    )


def positions(token, len_ref):
    end = jnp.int32(0)
    segment = jnp.zeros_like(token)
    start = jnp.zeros_like(token)
    for i in range(len_ref.shape[0]):
        end = end + len_ref[i]
        past = token >= end
        segment = segment + past.astype(jnp.int32)
        start = start + jnp.where(past, len_ref[i], 0)
    return segment, token - start


def tables_kernel(*refs, rows, spans):
    n = len(spans)
    sources, (turn_ref, allow_ref), targets, (sems, len_ref, len_sem) = refs[: n + 1], refs[n + 1 : n + 3], refs[n + 3 : -3], refs[-3:]
    lengths = pltpu.make_async_copy(sources[0], len_ref, len_sem)
    lengths.start()
    copies = fetches(sources[1:], targets, spans, sems)
    for copy in copies:
        copy.start()
    me = lax.axis_index("wide")
    total, dim = turn_ref.shape[1:]

    def owner(row, base):
        return rows * jnp.bitwise_xor(row // rows, base) + lax.rem(row, rows)

    shape = (total, dim)
    power = lax.rem(lax.broadcasted_iota(jnp.int32, shape, 1), dim // 2).astype(F32)
    freq = jnp.exp(power * F32(-2.0 * math.log(theta_base) / dim))
    lengths.wait()
    row = lax.broadcasted_iota(jnp.int32, shape, 0)
    lane = lax.broadcasted_iota(jnp.int32, shape, 1)
    for i, base in enumerate((me, me // 2)):
        angle = positions(owner(row, base), len_ref)[1].astype(F32) * freq
        sine = jnp.sin(angle)
        turn_ref[2 * i] = jnp.cos(angle)
        turn_ref[2 * i + 1] = jnp.where(lane < dim // 2, -sine, sine)
    shape = allow_ref.shape
    query = owner(lax.rem(lax.broadcasted_iota(jnp.int32, shape, 0), total), me)
    key = owner(lax.broadcasted_iota(jnp.int32, shape, 1), me // 2)
    same = positions(query, len_ref)[0] == positions(key, len_ref)[0]
    allow_ref[...] = jnp.where(same & (key <= query), 1.0, 0.0).astype(F32)
    for copy in copies:
        copy.wait()


def join_kernel(*refs):
    for i, ref in enumerate(refs[:-1]):
        refs[-1][i] = ref[...]


def keyval_kernel(a_ref, b_ref, w_ref, *refs, order, spans):
    n = len(spans)
    sources, (x_out, keep_ref, give_ref), targets = refs[:n], refs[n : n + 3], refs[n + 3 : 2 * n + 3]
    x32, sems = refs[2 * n + 3 :]
    copies = fetches(sources, targets, spans, sems)
    for copy in copies:
        copy.start()
    count, rows = a_ref.shape[:2]
    for i in range(count):
        for base, ref in ((order[i], a_ref), (order[count + i], b_ref)):
            x32[rows * base : rows * (base + 1), :] = ref[i].astype(F32)
    x_out[...] = x32[...].astype(BF16)
    part = jnp.dot(x_out[...], w_ref[...], preferred_element_type=F32)
    width = keep_ref.shape[1]
    left, right = part[:, :width], part[:, width:]
    low = lax.axis_index("narrow") == 0
    keep_ref[...] = jnp.where(low, left, right)
    give_ref[...] = jnp.where(low, right, left)
    for copy in copies:
        copy.wait()


def pair_kernel(mine_ref, other_ref, out_ref):
    out_ref[...] = (mine_ref[...] + other_ref[...]).astype(BF16)


def multiply(x_ref, w_ref, out, at, lo=0, hi=None):
    width = (w_ref.shape[1] if hi is None else hi) - lo
    step = math.gcd(math.gcd(width, 512), lo)

    @pl.loop(0, width // step)
    def _(j):
        cols = pl.ds(pl.multiple_of(lo + j * step, step), step)
        part = jnp.dot(x_ref[...], w_ref[:, cols], preferred_element_type=F32)
        out[:, pl.ds(pl.multiple_of(at + j * step, step), step)] = part


def query_kernel(x_ref, w_ref, head_ref, *refs, spans):
    n = len(spans)
    sources, q_out, targets, sems = refs[:n], refs[n], refs[n + 1 : -1], refs[-1]
    copies = fetches(sources, targets, spans, sems)
    for copy in copies:
        copy.start()
    width = head_ref.shape[1]
    q_out[:, :width] = head_ref[...].astype(F32)
    multiply(x_ref, w_ref, q_out, width)
    for copy in copies:
        copy.wait()


def attend(mine_ref, other_ref, turn_ref, allow_ref, att):
    total, dim = turn_ref.shape[1:]
    low = lax.axis_index("narrow") == 0
    mine, other = mine_ref[:, :dim], other_ref[:, :dim]
    keys, values = jnp.where(low, mine, other), jnp.where(low, other, mine)
    summed = mine_ref[:, dim:] + other_ref[:, dim:]
    values = jnp.concatenate([values[total // 2 :], values[: total // 2]], axis=0).astype(BF16)

    def rotate(u, i):
        return (u * turn_ref[i] + pltpu.roll(u, dim // 2, 1) * turn_ref[i + 1]).astype(BF16)

    keys = rotate(keys, 2)
    heads = summed.shape[1] // dim
    stack = jnp.concatenate([rotate(summed[:, dim * h : dim * (h + 1)], 0) for h in range(heads)], axis=0)
    scores = lax.dot_general(stack, keys, (((1,), (1,)), ((), ())), preferred_element_type=F32)
    scores = scores / F32(math.sqrt(dim))
    scores = jnp.where(allow_ref[...] > 0, scores, F32(-1e30))
    weights = jnp.exp(scores - jnp.max(scores, axis=1, keepdims=True))
    probs = (weights / jnp.sum(weights, axis=1, keepdims=True)).astype(BF16)
    mixed = jnp.dot(probs, values, preferred_element_type=F32).astype(BF16)
    for h in range(heads):
        att[:, dim * h : dim * (h + 1)] = mixed[total * h : total * (h + 1), :]


def part_out(acc, keep_ref, send_ref):
    pieces = 2 * keep_ref.shape[0]
    rows = acc.shape[0] // pieces
    for s in range(0, pieces, 2):
        keep_ref[s // 2] = acc[rows * s : rows * (s + 1), :]
        send_ref[s // 2] = acc[rows * (s + 1) : rows * (s + 2), :].astype(BF16)


def output_kernel(*refs, first, parts, own, spans):
    n = len(spans)
    if first:
        head, refs = refs[:4], refs[4:]
    else:
        att, refs = refs[0], refs[1:]
    w_refs, refs = refs[:parts], refs[parts:]
    w_far = None
    if n or own:
        w_far, refs = refs[0], refs[1:]
    if first:
        att, refs = refs[0], refs[1:]
    keep_ref, send_ref, targets, refs = refs[0], refs[1], refs[2 : 2 + n], refs[2 + n :]
    acc, sems, mine = refs[0], refs[1], refs[2:]
    copies = fetches([w_far] * (len(own) + n), [*mine, *targets], [*own, *spans], sems)
    for copy in copies:
        copy.start()
    if first:
        attend(*head, att)
    at = 0
    for w_ref in w_refs:
        multiply(att, w_ref, acc, at)
        at += w_ref.shape[1]
    for copy, w_ref in zip(copies, mine):
        copy.wait()
        multiply(att, w_ref, acc, at)
        at += w_ref.shape[1]
    part_out(acc, keep_ref, send_ref)
    for copy in copies[len(own) :]:
        copy.wait()


def near_sum_kernel(*refs, parts):
    at = 0
    outs = refs[2 * parts :]
    for p in range(parts):
        keep_ref, got_ref = refs[2 * p : 2 * p + 2]
        width = keep_ref.shape[2]
        for k in range(keep_ref.shape[0]):
            part = keep_ref[k] + got_ref[k].astype(F32)
            outs[k][:, at : at + width] = part.astype(outs[k].dtype)
        at += width


def total_kernel(*refs):
    total = refs[0][...]
    for r in refs[1:-1]:
        total = total + r[...].astype(F32)
    refs[-1][...] = total.astype(BF16)


def swap(x, axis, size, bit):
    return lax.ppermute(x, axis, [(i, i ^ bit) for i in range(size)])


def shaped(*shape, dtype=F32):
    return jax.ShapeDtypeStruct(shape, dtype)


def plain_positions(lengths, total):
    index = jnp.arange(total, dtype=jnp.int32)
    ends = jnp.cumsum(lengths)
    past = index[:, None] >= ends[None, :]
    segment = jnp.sum(past.astype(jnp.int32), axis=1)
    offset = index - jnp.sum(jnp.where(past, lengths[None, :], 0), axis=1)
    return segment, offset


def plain_rotate(values, offset):
    half = values.shape[-1] // 2
    freq = theta_base ** (-(jnp.arange(half, dtype=F32) * 2.0) / values.shape[-1])
    angle = offset.astype(F32)[:, None] * freq[None, :]
    cosine = jnp.cos(angle)[:, None, :]
    sine = jnp.sin(angle)[:, None, :]
    first, second = values[..., :half], values[..., half:]
    return jnp.concatenate([first * cosine - second * sine, second * cosine + first * sine], axis=-1)


def plain_attend(query, keys, values, segment):
    total = query.shape[0]
    scores = jnp.einsum("qhd,khd->hqk", query, keys, preferred_element_type=F32) / jnp.sqrt(F32(query.shape[-1]))
    index = jnp.arange(total, dtype=jnp.int32)
    allowed = (segment[:, None] == segment[None, :]) & (index[None, :] <= index[:, None])
    scores = jnp.where(allowed[None], scores, F32(-1e30))
    weights = jnp.exp(scores - jnp.max(scores, axis=-1, keepdims=True))
    probs = (weights / jnp.sum(weights, axis=-1, keepdims=True)).astype(BF16)
    return jnp.einsum("hqk,khd->qhd", probs, values, preferred_element_type=F32).astype(BF16)


def plain(tokens, lengths, w_query, w_keyval, w_out):
    q_cols = w_query.shape[1]
    heads = q_cols // HEAD_DIM
    piece = lax.all_gather(tokens, "wide", axis=0, tiled=True)
    query_part = jnp.dot(piece, w_query, preferred_element_type=F32)
    keyval_part = jnp.dot(piece, w_keyval, preferred_element_type=F32)
    total = piece.shape[0]
    query = lax.psum(query_part, "narrow")
    summed = lax.psum(keyval_part, "narrow").astype(BF16)
    keyval = lax.all_gather(summed, "wide", axis=1, tiled=True)
    segment, offset = plain_positions(lengths, total)
    kv_width = KV_HEADS * HEAD_DIM
    keys = plain_rotate(keyval[:, :kv_width].astype(F32).reshape(total, KV_HEADS, HEAD_DIM), offset).astype(BF16)
    values = keyval[:, kv_width:].reshape(total, KV_HEADS, HEAD_DIM)
    head_ids = lax.axis_index("wide") * heads + jnp.arange(heads, dtype=jnp.int32)
    kv_ids = head_ids // (HEADS // KV_HEADS)
    query_rot = plain_rotate(query.reshape(total, -1, HEAD_DIM), offset).astype(BF16)
    attended = plain_attend(query_rot, jnp.take(keys, kv_ids, axis=1), jnp.take(values, kv_ids, axis=1), segment)
    mixed = lax.psum_scatter(
        jnp.dot(attended.reshape(total, -1), w_out, preferred_element_type=F32), "wide", scatter_dimension=0, tiled=True
    )
    return mixed.astype(BF16)


def local(tokens, lengths, w_query, w_keyval, w_out):
    wide = lax.axis_size("wide")
    rows, depth = tokens.shape
    total = rows * wide
    kv_cols, q_cols, out_cols = w_keyval.shape[1], w_query.shape[1], w_out.shape[1]
    heads = q_cols // HEAD_DIM

    o_cuts = [out_cols * k // 32 for k in CUTS]
    o_near, spans = [], [(o_cuts[0], o_cuts[1])]
    along = list(reversed(range(2, wide, 2)))
    others = [swap(tokens, "wide", wide, bit) for bit in along]
    turn, allow, w = call(
        functools.partial(tables_kernel, rows=rows, spans=spans),
        "tables",
        [lengths, w_out],
        [shaped(4, total, HEAD_DIM), shaped(heads * total, total)] + [fetched(w_out, *s) for s in spans],
        [pltpu.SemaphoreType.DMA((1,)), pltpu.SMEM(lengths.shape, jnp.int32), pltpu.SemaphoreType.DMA],
        limit=2,
        far=2,
        hint=HINT,
    )
    o_near.append(w)
    order = [*along, 0]
    (x,) = call(
        join_kernel, "join", [*others, tokens], [shaped(len(order), rows, depth, dtype=BF16)], limit=2, after=[turn], hint=JH[0]
    )
    order = order + [s ^ 1 for s in order]
    other = swap(x, "wide", wide, 1)
    if o_cuts[3] > o_cuts[1]:
        (w,) = ahead("ahead1", [w_out], [(o_cuts[1], o_cuts[3])], after=[x])
        o_near.append(w)
    x, keep, give = call(
        functools.partial(keyval_kernel, order=order, spans=[]),
        "keyval",
        [x, other, near(w_keyval)],
        [shaped(total, depth, dtype=BF16)] + [shaped(total, HEAD_DIM)] * 2,
        [pltpu.VMEM((total, depth), F32), pltpu.SemaphoreType.DMA((1,))],
        limit=4,
        hint=KH,
        after=[o_near[-1]],
    )

    half = wide // 2
    given = swap(give, "narrow", 2, 1)
    (head,) = call(pair_kernel, "pair", [keep, given], [shaped(total, HEAD_DIM, dtype=BF16)], limit=1)
    routes = [(2 * s + n, 2 * ((2 * s + n) % wide) + s // half) for s in range(wide) for n in range(2)]
    sent = head
    head = lax.ppermute(head, ("wide", "narrow"), routes)
    if o_cuts[4] > o_cuts[3]:
        (w,) = ahead("ahead3", [w_out], [(o_cuts[3], o_cuts[4])], after=[sent])
        o_near.append(w)
    unit = out_cols * QSTEP // 32
    spans = [(lo, min(lo + unit, o_cuts[5])) for lo in range(o_cuts[4], o_cuts[5], unit)]
    q, *pieces = call(
        functools.partial(query_kernel, spans=spans),
        "query",
        [x, near(w_query), head] + [w_out] * len(spans),
        [QOUT((total, q_cols + HEAD_DIM), F32)] + [fetched(w_out, *span) for span in spans],
        [pltpu.SemaphoreType.DMA((len(spans),))],
        limit=2,
        far=len(spans),
        after=o_near[-1:],
    )
    o_near += pieces
    other = swap(q, "narrow", 2, 1)
    if o_cuts[6] > o_cuts[5]:
        (w,) = ahead("ahead4", [w_out], [(o_cuts[5], o_cuts[6])], after=[q])
        o_near.append(w)

    def output(name, head, weights, own, spans):
        own_cols = [hi - lo for lo, hi in own]
        width = sum(w.shape[1] for w in weights) + sum(own_cols)
        return call(
            functools.partial(output_kernel, first=len(head) > 1, parts=len(weights), own=own, spans=spans),
            name,
            [*head, *[near(w) for w in weights], *([w_out] if own or spans else [])],
            ([shaped(total, q_cols, dtype=BF16)] if len(head) > 1 else [])
            + [shaped(wide // 2, rows, width), shaped(wide // 2, rows, width, dtype=BF16)]
            + [fetched(w_out, *span) for span in spans],
            [pltpu.VMEM((total, width), F32), pltpu.SemaphoreType.DMA((max(1, len(own) + len(spans)),))]
            + [pltpu.VMEM((w_out.shape[0], cols), BF16) for cols in own_cols],
            limit=LIM,
            far=1 if own or spans else 0,
        )

    att, keep0, send0, o2 = output(
        "output0",
        [q, other, turn, allow],
        o_near,
        [span for span in [(o_cuts[6], o_cuts[7])] if span[1] > span[0]],
        [(o_cuts[7], o_cuts[8])],
    )
    got0 = swap(send0, "wide", wide, 1)
    keep1, send1 = output("output1", [att], [o2], [], [])
    got1 = swap(send1, "wide", wide, 1)
    mine, *others = call(
        functools.partial(near_sum_kernel, parts=2),
        "pairs",
        [keep0, got0, keep1, got1],
        [shaped(rows, out_cols)] + [shaped(rows, out_cols, dtype=BF16)] * (half - 1),
        limit=1,
    )
    back = {k: swap(others[k - 1], "wide", wide, 2 * k) for k in reversed(range(1, half))}
    return call(total_kernel, "total", [mine] + [back[k] for k in reversed(range(1, half))], [shaped(rows, out_cols, dtype=BF16)], limit=1)[0]


def solution(mesh):
    in_specs = (
        P(("groups", "wide"), "narrow"),
        P("groups"),
        P("narrow", "wide"),
        P("narrow", "wide"),
        P("wide", "narrow"),
    )
    out_specs = P(("groups", "wide"), "narrow")
    body = local if mesh.shape["wide"] == KV_HEADS and mesh.shape["narrow"] == 2 else plain
    return jax.shard_map(body, mesh=mesh, in_specs=in_specs, out_specs=out_specs, check_vma=False)
```

```python
import functools
import math

import jax
import jax.numpy as jnp
from jax import lax
from jax.experimental import pallas as pl
from jax.experimental.pallas import tpu as pltpu
from jax.sharding import PartitionSpec as P

HEADS = 128
KV_HEADS = 8
HEAD_DIM = 128
theta_base = 500000.0
F32 = jnp.float32
BF16 = jnp.bfloat16
MIB = 1 << 20
CUTS = (0, 4, 4, 4, 5, 18, 20, 20, 32)
QSTEP = 4
QOUT = pltpu.VMEM
LIM = 6
HINT = 0
JH = (0, 0)
KH = 0


def vspec():
    return pl.BlockSpec(memory_space=pltpu.VMEM)


def aspec():
    return pl.BlockSpec(memory_space=pltpu.HBM)


def near(x):
    return pltpu.with_memory_space_constraint(x, pltpu.VMEM)


def call(kernel, name, ins, outs, scratch=(), limit=4, far=0, hint=0, smem=0, after=(), behind=()):
    if after:
        inner, skip = kernel, len(after)
        kernel = lambda *refs: inner(*refs[skip:])
        ins = [*[near(x) for x in after], *ins]
    if behind:
        whole, drop, keep = kernel, len(behind), len(ins) + len(after)
        kernel = lambda *refs: whole(*refs[:keep], *refs[keep + drop :])
        ins, far = [*ins, *behind], far + drop
    if far:
        ins = [*ins[:-far], *[pltpu.with_memory_space_constraint(x, pltpu.HBM) for x in ins[-far:]]]
    specs = [pl.BlockSpec(memory_space=pltpu.SMEM)] * smem
    specs += [vspec()] * (len(ins) - smem - far) + [aspec()] * far
    return pl.pallas_call(
        kernel,
        out_shape=tuple(outs),
        in_specs=specs,
        out_specs=(vspec(),) * len(outs),
        scratch_shapes=list(scratch),
        compiler_params=pltpu.CompilerParams(vmem_limit_bytes=limit * MIB),
        cost_estimate=pl.CostEstimate(flops=hint, bytes_accessed=1000, transcendentals=0),
        name=name,
    )(*ins)


def fetched(w, lo, hi):
    return pltpu.VMEM((w.shape[0], hi - lo), BF16)


def fetches(sources, targets, spans, sems):
    return [
        pltpu.make_async_copy(src.at[:, pl.ds(lo, hi - lo)], dst, sems.at[i])
        for i, (src, dst, (lo, hi)) in enumerate(zip(sources, targets, spans))
    ]


def ahead_kernel(*refs, spans):
    n = len(spans)
    copies = fetches(refs[:n], refs[n : 2 * n], spans, refs[-1])
    for copy in copies:
        copy.start()
    for copy in copies:
        copy.wait()


def ahead(name, sources, spans, after=(), behind=(), hint=0):
    return call(
        functools.partial(ahead_kernel, spans=spans),
        name,
        sources,
        [fetched(w, lo, hi) for w, (lo, hi) in zip(sources, spans)],
        [pltpu.SemaphoreType.DMA((len(spans),))],
        limit=1,
        far=len(sources),
        hint=hint,
        after=after,
        behind=behind,
    )


def positions(token, len_ref):
    end = jnp.int32(0)
    segment = jnp.zeros_like(token)
    start = jnp.zeros_like(token)
    for i in range(len_ref.shape[0]):
        end = end + len_ref[i]
        past = token >= end
        segment = segment + past.astype(jnp.int32)
        start = start + jnp.where(past, len_ref[i], 0)
    return segment, token - start


def tables_kernel(*refs, rows, spans):
    n = len(spans)
    sources, (turn_ref, allow_ref), targets, (sems, len_ref, len_sem) = refs[: n + 1], refs[n + 1 : n + 3], refs[n + 3 : -3], refs[-3:]
    lengths = pltpu.make_async_copy(sources[0], len_ref, len_sem)
    lengths.start()
    copies = fetches(sources[1:], targets, spans, sems)
    for copy in copies:
        copy.start()
    me = lax.axis_index("wide")
    total, dim = turn_ref.shape[1:]

    def owner(row, base):
        return rows * jnp.bitwise_xor(row // rows, base) + lax.rem(row, rows)

    shape = (total, dim)
    power = lax.rem(lax.broadcasted_iota(jnp.int32, shape, 1), dim // 2).astype(F32)
    freq = jnp.exp(power * F32(-2.0 * math.log(theta_base) / dim))
    lengths.wait()
    row = lax.broadcasted_iota(jnp.int32, shape, 0)
    lane = lax.broadcasted_iota(jnp.int32, shape, 1)
    for i, base in enumerate((me, me // 2)):
        angle = positions(owner(row, base), len_ref)[1].astype(F32) * freq
        sine = jnp.sin(angle)
        turn_ref[2 * i] = jnp.cos(angle)
        turn_ref[2 * i + 1] = jnp.where(lane < dim // 2, -sine, sine)
    shape = allow_ref.shape
    query = owner(lax.rem(lax.broadcasted_iota(jnp.int32, shape, 0), total), me)
    key = owner(lax.broadcasted_iota(jnp.int32, shape, 1), me // 2)
    same = positions(query, len_ref)[0] == positions(key, len_ref)[0]
    allow_ref[...] = jnp.where(same & (key <= query), 1.0, 0.0).astype(F32)
    for copy in copies:
        copy.wait()


def join_kernel(*refs):
    for i, ref in enumerate(refs[:-1]):
        refs[-1][i] = ref[...]


def keyval_kernel(a_ref, b_ref, w_ref, *refs, order, spans):
    n = len(spans)
    sources, (x_out, keep_ref, give_ref), targets = refs[:n], refs[n : n + 3], refs[n + 3 : 2 * n + 3]
    x32, sems = refs[2 * n + 3 :]
    copies = fetches(sources, targets, spans, sems)
    for copy in copies:
        copy.start()
    count, rows = a_ref.shape[:2]
    for i in range(count):
        for base, ref in ((order[i], a_ref), (order[count + i], b_ref)):
            x32[rows * base : rows * (base + 1), :] = ref[i].astype(F32)
    x_out[...] = x32[...].astype(BF16)
    part = jnp.dot(x_out[...], w_ref[...], preferred_element_type=F32)
    width = keep_ref.shape[1]
    left, right = part[:, :width], part[:, width:]
    low = lax.axis_index("narrow") == 0
    keep_ref[...] = jnp.where(low, left, right)
    give_ref[...] = jnp.where(low, right, left)
    for copy in copies:
        copy.wait()


def pair_kernel(mine_ref, other_ref, out_ref):
    out_ref[...] = (mine_ref[...] + other_ref[...]).astype(BF16)


def multiply(x_ref, w_ref, out, at, lo=0, hi=None):
    width = (w_ref.shape[1] if hi is None else hi) - lo
    step = math.gcd(math.gcd(width, 512), lo)

    @pl.loop(0, width // step)
    def _(j):
        cols = pl.ds(pl.multiple_of(lo + j * step, step), step)
        part = jnp.dot(x_ref[...], w_ref[:, cols], preferred_element_type=F32)
        out[:, pl.ds(pl.multiple_of(at + j * step, step), step)] = part


def query_kernel(x_ref, w_ref, *refs, spans):
    n = len(spans)
    sources, q_out, targets, sems = refs[:n], refs[n], refs[n + 1 : -1], refs[-1]
    copies = fetches(sources, targets, spans, sems)
    for copy in copies:
        copy.start()
    multiply(x_ref, w_ref, q_out, 0)
    for copy in copies:
        copy.wait()


def pack_kernel(*refs):
    at = 0
    for ref in refs[:-1]:
        refs[-1][:, at : at + ref.shape[1]] = ref[...].astype(F32)
        at += ref.shape[1]


def attend(mine_ref, other_ref, turn_ref, allow_ref, att):
    total, dim = turn_ref.shape[1:]
    low = lax.axis_index("narrow") == 0
    mine, other = mine_ref[:, :dim], other_ref[:, :dim]
    keys, values = jnp.where(low, mine, other), jnp.where(low, other, mine)
    summed = mine_ref[:, dim:] + other_ref[:, dim:]
    values = jnp.concatenate([values[total // 2 :], values[: total // 2]], axis=0).astype(BF16)

    def rotate(u, i):
        return (u * turn_ref[i] + pltpu.roll(u, dim // 2, 1) * turn_ref[i + 1]).astype(BF16)

    keys = rotate(keys, 2)
    heads = summed.shape[1] // dim
    stack = jnp.concatenate([rotate(summed[:, dim * h : dim * (h + 1)], 0) for h in range(heads)], axis=0)
    scores = lax.dot_general(stack, keys, (((1,), (1,)), ((), ())), preferred_element_type=F32)
    scores = scores / F32(math.sqrt(dim))
    scores = jnp.where(allow_ref[...] > 0, scores, F32(-1e30))
    weights = jnp.exp(scores - jnp.max(scores, axis=1, keepdims=True))
    probs = (weights / jnp.sum(weights, axis=1, keepdims=True)).astype(BF16)
    mixed = jnp.dot(probs, values, preferred_element_type=F32).astype(BF16)
    for h in range(heads):
        att[:, dim * h : dim * (h + 1)] = mixed[total * h : total * (h + 1), :]


def part_out(acc, keep_ref, send_ref):
    pieces = 2 * keep_ref.shape[0]
    rows = acc.shape[0] // pieces
    for s in range(0, pieces, 2):
        keep_ref[s // 2] = acc[rows * s : rows * (s + 1), :]
        send_ref[s // 2] = acc[rows * (s + 1) : rows * (s + 2), :].astype(BF16)


def output_kernel(*refs, first, parts, own, spans):
    n = len(spans)
    if first:
        head, refs = refs[:4], refs[4:]
    else:
        att, refs = refs[0], refs[1:]
    w_refs, refs = refs[:parts], refs[parts:]
    w_far = None
    if n or own:
        w_far, refs = refs[0], refs[1:]
    if first:
        att, refs = refs[0], refs[1:]
    keep_ref, send_ref, targets, refs = refs[0], refs[1], refs[2 : 2 + n], refs[2 + n :]
    acc, sems, mine = refs[0], refs[1], refs[2:]
    copies = fetches([w_far] * (len(own) + n), [*mine, *targets], [*own, *spans], sems)
    for copy in copies:
        copy.start()
    if first:
        attend(*head, att)
    at = 0
    for w_ref in w_refs:
        multiply(att, w_ref, acc, at)
        at += w_ref.shape[1]
    for copy, w_ref in zip(copies, mine):
        copy.wait()
        multiply(att, w_ref, acc, at)
        at += w_ref.shape[1]
    part_out(acc, keep_ref, send_ref)
    for copy in copies[len(own) :]:
        copy.wait()


def near_sum_kernel(*refs, parts):
    at = 0
    outs = refs[2 * parts :]
    for p in range(parts):
        keep_ref, got_ref = refs[2 * p : 2 * p + 2]
        width = keep_ref.shape[2]
        for k in range(keep_ref.shape[0]):
            part = keep_ref[k] + got_ref[k].astype(F32)
            outs[k][:, at : at + width] = part.astype(outs[k].dtype)
        at += width


def total_kernel(*refs):
    total = refs[0][...]
    for r in refs[1:-1]:
        total = total + r[...].astype(F32)
    refs[-1][...] = total.astype(BF16)


def swap(x, axis, size, bit):
    return lax.ppermute(x, axis, [(i, i ^ bit) for i in range(size)])


def shaped(*shape, dtype=F32):
    return jax.ShapeDtypeStruct(shape, dtype)


def plain_positions(lengths, total):
    index = jnp.arange(total, dtype=jnp.int32)
    ends = jnp.cumsum(lengths)
    past = index[:, None] >= ends[None, :]
    segment = jnp.sum(past.astype(jnp.int32), axis=1)
    offset = index - jnp.sum(jnp.where(past, lengths[None, :], 0), axis=1)
    return segment, offset


def plain_rotate(values, offset):
    half = values.shape[-1] // 2
    freq = theta_base ** (-(jnp.arange(half, dtype=F32) * 2.0) / values.shape[-1])
    angle = offset.astype(F32)[:, None] * freq[None, :]
    cosine = jnp.cos(angle)[:, None, :]
    sine = jnp.sin(angle)[:, None, :]
    first, second = values[..., :half], values[..., half:]
    return jnp.concatenate([first * cosine - second * sine, second * cosine + first * sine], axis=-1)


def plain_attend(query, keys, values, segment):
    total = query.shape[0]
    scores = jnp.einsum("qhd,khd->hqk", query, keys, preferred_element_type=F32) / jnp.sqrt(F32(query.shape[-1]))
    index = jnp.arange(total, dtype=jnp.int32)
    allowed = (segment[:, None] == segment[None, :]) & (index[None, :] <= index[:, None])
    scores = jnp.where(allowed[None], scores, F32(-1e30))
    weights = jnp.exp(scores - jnp.max(scores, axis=-1, keepdims=True))
    probs = (weights / jnp.sum(weights, axis=-1, keepdims=True)).astype(BF16)
    return jnp.einsum("hqk,khd->qhd", probs, values, preferred_element_type=F32).astype(BF16)


def plain(tokens, lengths, w_query, w_keyval, w_out):
    q_cols = w_query.shape[1]
    heads = q_cols // HEAD_DIM
    piece = lax.all_gather(tokens, "wide", axis=0, tiled=True)
    query_part = jnp.dot(piece, w_query, preferred_element_type=F32)
    keyval_part = jnp.dot(piece, w_keyval, preferred_element_type=F32)
    total = piece.shape[0]
    query = lax.psum(query_part, "narrow")
    summed = lax.psum(keyval_part, "narrow").astype(BF16)
    keyval = lax.all_gather(summed, "wide", axis=1, tiled=True)
    segment, offset = plain_positions(lengths, total)
    kv_width = KV_HEADS * HEAD_DIM
    keys = plain_rotate(keyval[:, :kv_width].astype(F32).reshape(total, KV_HEADS, HEAD_DIM), offset).astype(BF16)
    values = keyval[:, kv_width:].reshape(total, KV_HEADS, HEAD_DIM)
    head_ids = lax.axis_index("wide") * heads + jnp.arange(heads, dtype=jnp.int32)
    kv_ids = head_ids // (HEADS // KV_HEADS)
    query_rot = plain_rotate(query.reshape(total, -1, HEAD_DIM), offset).astype(BF16)
    attended = plain_attend(query_rot, jnp.take(keys, kv_ids, axis=1), jnp.take(values, kv_ids, axis=1), segment)
    mixed = lax.psum_scatter(
        jnp.dot(attended.reshape(total, -1), w_out, preferred_element_type=F32), "wide", scatter_dimension=0, tiled=True
    )
    return mixed.astype(BF16)


def local(tokens, lengths, w_query, w_keyval, w_out):
    wide = lax.axis_size("wide")
    rows, depth = tokens.shape
    total = rows * wide
    kv_cols, q_cols, out_cols = w_keyval.shape[1], w_query.shape[1], w_out.shape[1]
    heads = q_cols // HEAD_DIM

    o_cuts = [out_cols * k // 32 for k in CUTS]
    o_near, spans = [], [(o_cuts[0], o_cuts[1])]
    along = list(reversed(range(2, wide, 2)))
    others = [swap(tokens, "wide", wide, bit) for bit in along]
    turn, allow, w = call(
        functools.partial(tables_kernel, rows=rows, spans=spans),
        "tables",
        [lengths, w_out],
        [shaped(4, total, HEAD_DIM), shaped(heads * total, total)] + [fetched(w_out, *s) for s in spans],
        [pltpu.SemaphoreType.DMA((1,)), pltpu.SMEM(lengths.shape, jnp.int32), pltpu.SemaphoreType.DMA],
        limit=2,
        far=2,
        hint=HINT,
    )
    o_near.append(w)
    order = [*along, 0]
    (x,) = call(
        join_kernel, "join", [*others, tokens], [shaped(len(order), rows, depth, dtype=BF16)], limit=2, after=[turn], hint=JH[0]
    )
    order = order + [s ^ 1 for s in order]
    other = swap(x, "wide", wide, 1)
    if o_cuts[3] > o_cuts[1]:
        (w,) = ahead("ahead1", [w_out], [(o_cuts[1], o_cuts[3])], after=[x])
        o_near.append(w)
    x, keep, give = call(
        functools.partial(keyval_kernel, order=order, spans=[]),
        "keyval",
        [x, other, near(w_keyval)],
        [shaped(total, depth, dtype=BF16)] + [shaped(total, HEAD_DIM)] * 2,
        [pltpu.VMEM((total, depth), F32), pltpu.SemaphoreType.DMA((1,))],
        limit=4,
        hint=KH,
        after=[o_near[-1]],
    )

    half = wide // 2
    given = swap(give, "narrow", 2, 1)
    (w,) = ahead("ahead3", [w_out], [(o_cuts[3], o_cuts[4])], after=[keep])
    o_near.append(w)
    (head,) = call(pair_kernel, "pair", [keep, given], [shaped(total, HEAD_DIM, dtype=BF16)], limit=1, after=[w])
    routes = [(2 * s + n, 2 * ((2 * s + n) % wide) + s // half) for s in range(wide) for n in range(2)]
    sent = head
    head = lax.ppermute(head, ("wide", "narrow"), routes)
    unit = out_cols * QSTEP // 32
    spans = [(lo, min(lo + unit, o_cuts[5])) for lo in range(o_cuts[4], o_cuts[5], unit)]
    q, *pieces = call(
        functools.partial(query_kernel, spans=spans),
        "query",
        [x, near(w_query)] + [w_out] * len(spans),
        [shaped(total, q_cols)] + [fetched(w_out, *span) for span in spans],
        [pltpu.SemaphoreType.DMA((len(spans),))],
        limit=2,
        far=len(spans),
        after=[sent],
    )
    o_near += pieces
    (q,) = call(pack_kernel, "pack", [head, q], [shaped(total, HEAD_DIM + q_cols)], limit=1)
    other = swap(q, "narrow", 2, 1)
    if o_cuts[6] > o_cuts[5]:
        (w,) = ahead("ahead4", [w_out], [(o_cuts[5], o_cuts[6])], after=[q])
        o_near.append(w)

    def output(name, head, weights, own, spans):
        own_cols = [hi - lo for lo, hi in own]
        width = sum(w.shape[1] for w in weights) + sum(own_cols)
        return call(
            functools.partial(output_kernel, first=len(head) > 1, parts=len(weights), own=own, spans=spans),
            name,
            [*head, *[near(w) for w in weights], *([w_out] if own or spans else [])],
            ([shaped(total, q_cols, dtype=BF16)] if len(head) > 1 else [])
            + [shaped(wide // 2, rows, width), shaped(wide // 2, rows, width, dtype=BF16)]
            + [fetched(w_out, *span) for span in spans],
            [pltpu.VMEM((total, width), F32), pltpu.SemaphoreType.DMA((max(1, len(own) + len(spans)),))]
            + [pltpu.VMEM((w_out.shape[0], cols), BF16) for cols in own_cols],
            limit=LIM,
            far=1 if own or spans else 0,
        )

    att, keep0, send0, o2 = output(
        "output0",
        [q, other, turn, allow],
        o_near,
        [span for span in [(o_cuts[6], o_cuts[7])] if span[1] > span[0]],
        [(o_cuts[7], o_cuts[8])],
    )
    got0 = swap(send0, "wide", wide, 1)
    keep1, send1 = output("output1", [att], [o2], [], [])
    got1 = swap(send1, "wide", wide, 1)
    mine, *others = call(
        functools.partial(near_sum_kernel, parts=2),
        "pairs",
        [keep0, got0, keep1, got1],
        [shaped(rows, out_cols)] + [shaped(rows, out_cols, dtype=BF16)] * (half - 1),
        limit=1,
    )
    back = {k: swap(others[k - 1], "wide", wide, 2 * k) for k in reversed(range(1, half))}
    return call(total_kernel, "total", [mine] + [back[k] for k in reversed(range(1, half))], [shaped(rows, out_cols, dtype=BF16)], limit=1)[0]


def solution(mesh):
    in_specs = (
        P(("groups", "wide"), "narrow"),
        P("groups"),
        P("narrow", "wide"),
        P("narrow", "wide"),
        P("wide", "narrow"),
    )
    out_specs = P(("groups", "wide"), "narrow")
    body = local if mesh.shape["wide"] == KV_HEADS and mesh.shape["narrow"] == 2 else plain
    return jax.shard_map(body, mesh=mesh, in_specs=in_specs, out_specs=out_specs, check_vma=False)
```

```python
import functools
import math

import jax
import jax.numpy as jnp
from jax import lax
from jax.experimental import pallas as pl
from jax.experimental.pallas import tpu as pltpu
from jax.sharding import PartitionSpec as P

HEADS = 128
KV_HEADS = 8
HEAD_DIM = 128
theta_base = 500000.0
F32 = jnp.float32
BF16 = jnp.bfloat16
MIB = 1 << 20
CUTS = (0, 4, 16, 18, 24, 32)
STEP = 4
FILL = 9 * 10**9


def vspec():
    return pl.BlockSpec(memory_space=pltpu.VMEM)


def aspec():
    return pl.BlockSpec(memory_space=pltpu.HBM)


def near(x):
    return pltpu.with_memory_space_constraint(x, pltpu.VMEM)


def call(kernel, name, ins, outs, scratch=(), limit=4, far=0, hint=0, smem=0, after=(), behind=()):
    if after:
        inner, skip = kernel, len(after)
        kernel = lambda *refs: inner(*refs[skip:])
        ins = [*[near(x) for x in after], *ins]
    if behind:
        whole, drop, keep = kernel, len(behind), len(ins) + len(after)
        kernel = lambda *refs: whole(*refs[:keep], *refs[keep + drop :])
        ins, far = [*ins, *behind], far + drop
    if far:
        ins = [*ins[:-far], *[pltpu.with_memory_space_constraint(x, pltpu.HBM) for x in ins[-far:]]]
    specs = [pl.BlockSpec(memory_space=pltpu.SMEM)] * smem
    specs += [vspec()] * (len(ins) - smem - far) + [aspec()] * far
    return pl.pallas_call(
        kernel,
        out_shape=tuple(outs),
        in_specs=specs,
        out_specs=(vspec(),) * len(outs),
        scratch_shapes=list(scratch),
        compiler_params=pltpu.CompilerParams(vmem_limit_bytes=limit * MIB),
        cost_estimate=pl.CostEstimate(flops=hint, bytes_accessed=1000, transcendentals=0),
        name=name,
    )(*ins)


def fetched(w, lo, hi):
    return pltpu.VMEM((w.shape[0], hi - lo), BF16)


def fetches(sources, targets, spans, sems):
    return [
        pltpu.make_async_copy(src.at[:, pl.ds(lo, hi - lo)], dst, sems.at[i])
        for i, (src, dst, (lo, hi)) in enumerate(zip(sources, targets, spans))
    ]


def ahead_kernel(*refs, spans):
    n = len(spans)
    copies = fetches(refs[:n], refs[n : 2 * n], spans, refs[-1])
    for copy in copies:
        copy.start()
    for copy in copies:
        copy.wait()


def ahead(name, sources, spans, after=(), behind=(), hint=0):
    return call(
        functools.partial(ahead_kernel, spans=spans),
        name,
        sources,
        [fetched(w, lo, hi) for w, (lo, hi) in zip(sources, spans)],
        [pltpu.SemaphoreType.DMA((len(spans),))],
        limit=1,
        far=len(sources),
        hint=hint,
        after=after,
        behind=behind,
    )


def positions(token, len_ref):
    end = jnp.int32(0)
    segment = jnp.zeros_like(token)
    start = jnp.zeros_like(token)
    for i in range(len_ref.shape[0]):
        end = end + len_ref[i]
        past = token >= end
        segment = segment + past.astype(jnp.int32)
        start = start + jnp.where(past, len_ref[i], 0)
    return segment, token - start


def tables_kernel(*refs, rows, spans):
    n = len(spans)
    sources, (turn_ref, allow_ref), targets, (sems, len_ref, len_sem) = refs[: n + 1], refs[n + 1 : n + 3], refs[n + 3 : -3], refs[-3:]
    lengths = pltpu.make_async_copy(sources[0], len_ref, len_sem)
    lengths.start()
    copies = fetches(sources[1:], targets, spans, sems)
    for copy in copies:
        copy.start()
    me = lax.axis_index("wide")
    total, dim = turn_ref.shape[1:]

    def owner(row, base):
        return rows * jnp.bitwise_xor(row // rows, base) + lax.rem(row, rows)

    shape = (total, dim)
    power = lax.rem(lax.broadcasted_iota(jnp.int32, shape, 1), dim // 2).astype(F32)
    freq = jnp.exp(power * F32(-2.0 * math.log(theta_base) / dim))
    lengths.wait()
    row = lax.broadcasted_iota(jnp.int32, shape, 0)
    lane = lax.broadcasted_iota(jnp.int32, shape, 1)
    for i, base in enumerate((me, me // 2)):
        angle = positions(owner(row, base), len_ref)[1].astype(F32) * freq
        sine = jnp.sin(angle)
        turn_ref[2 * i] = jnp.cos(angle)
        turn_ref[2 * i + 1] = jnp.where(lane < dim // 2, -sine, sine)
    shape = allow_ref.shape
    query = owner(lax.rem(lax.broadcasted_iota(jnp.int32, shape, 0), total), me)
    key = owner(lax.broadcasted_iota(jnp.int32, shape, 1), me // 2)
    same = positions(query, len_ref)[0] == positions(key, len_ref)[0]
    allow_ref[...] = jnp.where(same & (key <= query), 1.0, 0.0).astype(F32)
    for copy in copies:
        copy.wait()


def join_kernel(*refs):
    for i, ref in enumerate(refs[:-1]):
        refs[-1][i] = ref[...]


def keyval_kernel(*refs, order, spans):
    n = len(spans)
    parts, w_ref, refs = refs[: len(order)], refs[len(order)], refs[len(order) + 1 :]
    sources, (x_out, keep_ref, give_ref), targets = refs[:n], refs[n : n + 3], refs[n + 3 : 2 * n + 3]
    x32, sems = refs[2 * n + 3 :]
    copies = fetches(sources, targets, spans, sems)
    for copy in copies:
        copy.start()
    rows = parts[0].shape[1]
    for ref, owners in zip(parts, order):
        for i, s in enumerate(owners):
            x32[rows * s : rows * (s + 1), :] = ref[i].astype(F32)
    x_out[...] = x32[...].astype(BF16)
    part = jnp.dot(x_out[...], w_ref[...], preferred_element_type=F32)
    width = keep_ref.shape[1]
    left, right = part[:, :width], part[:, width:]
    low = lax.axis_index("narrow") == 0
    keep_ref[...] = jnp.where(low, left, right)
    give_ref[...] = jnp.where(low, right, left)
    for copy in copies:
        copy.wait()


def pair_kernel(mine_ref, other_ref, out_ref):
    out_ref[...] = (mine_ref[...] + other_ref[...]).astype(BF16)


def multiply(x_ref, w_ref, out, at, lo=0, hi=None):
    width = (w_ref.shape[1] if hi is None else hi) - lo
    step = math.gcd(math.gcd(width, min(1024, (1 << 23) // w_ref.shape[0])), lo)

    @pl.loop(0, width // step)
    def _(j):
        cols = pl.ds(pl.multiple_of(lo + j * step, step), step)
        part = jnp.dot(x_ref[...], w_ref[:, cols], preferred_element_type=F32)
        out[:, pl.ds(pl.multiple_of(at + j * step, step), step)] = part


def query_kernel(x_ref, w_ref, *refs, spans):
    n = len(spans)
    sources, q_out, targets, sems = refs[:n], refs[n], refs[n + 1 : -1], refs[-1]
    copies = fetches(sources, targets, spans, sems)
    for copy in copies:
        copy.start()
    multiply(x_ref, w_ref, q_out, 0)
    for copy in copies:
        copy.wait()


def pack_kernel(*refs):
    at = 0
    for ref in refs[:-1]:
        refs[-1][:, at : at + ref.shape[1]] = ref[...].astype(F32)
        at += ref.shape[1]


def attend(mine_ref, other_ref, turn_ref, allow_ref, att):
    total, dim = turn_ref.shape[1:]
    low = lax.axis_index("narrow") == 0
    mine, other = mine_ref[:, :dim], other_ref[:, :dim]
    keys, values = jnp.where(low, mine, other), jnp.where(low, other, mine)
    summed = mine_ref[:, dim:] + other_ref[:, dim:]
    values = jnp.concatenate([values[total // 2 :], values[: total // 2]], axis=0).astype(BF16)

    def rotate(u, i):
        return (u * turn_ref[i] + pltpu.roll(u, dim // 2, 1) * turn_ref[i + 1]).astype(BF16)

    keys = rotate(keys, 2)
    heads = summed.shape[1] // dim
    stack = jnp.concatenate([rotate(summed[:, dim * h : dim * (h + 1)], 0) for h in range(heads)], axis=0)
    scores = lax.dot_general(stack, keys, (((1,), (1,)), ((), ())), preferred_element_type=F32)
    scores = scores / F32(math.sqrt(dim))
    scores = jnp.where(allow_ref[...] > 0, scores, F32(-1e30))
    weights = jnp.exp(scores - jnp.max(scores, axis=1, keepdims=True))
    probs = (weights / jnp.sum(weights, axis=1, keepdims=True)).astype(BF16)
    mixed = jnp.dot(probs, values, preferred_element_type=F32).astype(BF16)
    for h in range(heads):
        att[:, dim * h : dim * (h + 1)] = mixed[total * h : total * (h + 1), :]


def part_out(acc, keep_ref, send_ref):
    pieces = 2 * keep_ref.shape[0]
    rows = acc.shape[0] // pieces
    for s in range(0, pieces, 2):
        keep_ref[s // 2] = acc[rows * s : rows * (s + 1), :]
        send_ref[s // 2] = acc[rows * (s + 1) : rows * (s + 2), :].astype(BF16)


def output_kernel(*refs, first, parts, own, spans):
    n = len(spans)
    if first:
        head, refs = refs[:4], refs[4:]
    else:
        att, refs = refs[0], refs[1:]
    w_refs, refs = refs[:parts], refs[parts:]
    w_far = None
    if n or own:
        w_far, refs = refs[0], refs[1:]
    if first:
        att, refs = refs[0], refs[1:]
    keep_ref, send_ref, targets, refs = refs[0], refs[1], refs[2 : 2 + n], refs[2 + n :]
    acc, sems, mine = refs[0], refs[1], refs[2:]
    copies = fetches([w_far] * (len(own) + n), [*mine, *targets], [*own, *spans], sems)
    for copy in copies:
        copy.start()
    if first:
        attend(*head, att)
    at = 0
    for w_ref in w_refs:
        multiply(att, w_ref, acc, at)
        at += w_ref.shape[1]
    for copy, w_ref in zip(copies, mine):
        copy.wait()
        multiply(att, w_ref, acc, at)
        at += w_ref.shape[1]
    part_out(acc, keep_ref, send_ref)
    for copy in copies[len(own) :]:
        copy.wait()


def near_sum_kernel(*refs, parts):
    at = 0
    outs = refs[2 * parts :]
    for p in range(parts):
        keep_ref, got_ref = refs[2 * p : 2 * p + 2]
        width = keep_ref.shape[2]
        for k in range(keep_ref.shape[0]):
            part = keep_ref[k] + got_ref[k].astype(F32)
            outs[k][:, at : at + width] = part.astype(outs[k].dtype)
        at += width


def total_kernel(*refs):
    total = refs[0][...]
    for r in refs[1:-1]:
        total = total + r[...].astype(F32)
    refs[-1][...] = total.astype(BF16)


def swap(x, axis, size, bit):
    return lax.ppermute(x, axis, [(i, i ^ bit) for i in range(size)])


def shaped(*shape, dtype=F32):
    return jax.ShapeDtypeStruct(shape, dtype)


def plain_positions(lengths, total):
    index = jnp.arange(total, dtype=jnp.int32)
    ends = jnp.cumsum(lengths)
    past = index[:, None] >= ends[None, :]
    segment = jnp.sum(past.astype(jnp.int32), axis=1)
    offset = index - jnp.sum(jnp.where(past, lengths[None, :], 0), axis=1)
    return segment, offset


def plain_rotate(values, offset):
    half = values.shape[-1] // 2
    freq = theta_base ** (-(jnp.arange(half, dtype=F32) * 2.0) / values.shape[-1])
    angle = offset.astype(F32)[:, None] * freq[None, :]
    cosine = jnp.cos(angle)[:, None, :]
    sine = jnp.sin(angle)[:, None, :]
    first, second = values[..., :half], values[..., half:]
    return jnp.concatenate([first * cosine - second * sine, second * cosine + first * sine], axis=-1)


def plain_attend(query, keys, values, segment):
    total = query.shape[0]
    scores = jnp.einsum("qhd,khd->hqk", query, keys, preferred_element_type=F32) / jnp.sqrt(F32(query.shape[-1]))
    index = jnp.arange(total, dtype=jnp.int32)
    allowed = (segment[:, None] == segment[None, :]) & (index[None, :] <= index[:, None])
    scores = jnp.where(allowed[None], scores, F32(-1e30))
    weights = jnp.exp(scores - jnp.max(scores, axis=-1, keepdims=True))
    probs = (weights / jnp.sum(weights, axis=-1, keepdims=True)).astype(BF16)
    return jnp.einsum("hqk,khd->qhd", probs, values, preferred_element_type=F32).astype(BF16)


def plain(tokens, lengths, w_query, w_keyval, w_out):
    q_cols = w_query.shape[1]
    heads = q_cols // HEAD_DIM
    piece = lax.all_gather(tokens, "wide", axis=0, tiled=True)
    query_part = jnp.dot(piece, w_query, preferred_element_type=F32)
    keyval_part = jnp.dot(piece, w_keyval, preferred_element_type=F32)
    total = piece.shape[0]
    query = lax.psum(query_part, "narrow")
    summed = lax.psum(keyval_part, "narrow").astype(BF16)
    keyval = lax.all_gather(summed, "wide", axis=1, tiled=True)
    segment, offset = plain_positions(lengths, total)
    kv_width = KV_HEADS * HEAD_DIM
    keys = plain_rotate(keyval[:, :kv_width].astype(F32).reshape(total, KV_HEADS, HEAD_DIM), offset).astype(BF16)
    values = keyval[:, kv_width:].reshape(total, KV_HEADS, HEAD_DIM)
    head_ids = lax.axis_index("wide") * heads + jnp.arange(heads, dtype=jnp.int32)
    kv_ids = head_ids // (HEADS // KV_HEADS)
    query_rot = plain_rotate(query.reshape(total, -1, HEAD_DIM), offset).astype(BF16)
    attended = plain_attend(query_rot, jnp.take(keys, kv_ids, axis=1), jnp.take(values, kv_ids, axis=1), segment)
    mixed = lax.psum_scatter(
        jnp.dot(attended.reshape(total, -1), w_out, preferred_element_type=F32), "wide", scatter_dimension=0, tiled=True
    )
    return mixed.astype(BF16)


def local(tokens, lengths, w_query, w_keyval, w_out):
    wide = lax.axis_size("wide")
    rows, depth = tokens.shape
    total = rows * wide
    kv_cols, q_cols, out_cols = w_keyval.shape[1], w_query.shape[1], w_out.shape[1]
    heads = q_cols // HEAD_DIM

    o_cuts = [out_cols * k // 32 for k in CUTS]
    o_near, spans = [], [(o_cuts[0], o_cuts[1])]
    along = list(reversed(range(2, wide, 2)))
    other = swap(tokens, "wide", wide, 1)
    turn, allow, w = call(
        functools.partial(tables_kernel, rows=rows, spans=spans),
        "tables",
        [lengths, w_out],
        [shaped(4, total, HEAD_DIM), shaped(heads * total, total)] + [fetched(w_out, *s) for s in spans],
        [pltpu.SemaphoreType.DMA((1,)), pltpu.SMEM(lengths.shape, jnp.int32), pltpu.SemaphoreType.DMA],
        limit=2,
        far=2,
    )
    o_near.append(w)
    (pair,) = call(join_kernel, "join", [tokens, other], [shaped(2, rows, depth, dtype=BF16)], limit=2, after=[turn])
    others = [swap(pair, "wide", wide, bit) for bit in along]
    others, along = others[::-1], along[::-1]
    order = [[bit, bit ^ 1] for bit in [*along, 0]]
    x, keep, give = call(
        functools.partial(keyval_kernel, order=order, spans=[]),
        "keyval",
        [*others, pair, near(w_keyval)],
        [shaped(total, depth, dtype=BF16)] + [shaped(total, HEAD_DIM)] * 2,
        [pltpu.VMEM((total, depth), F32), pltpu.SemaphoreType.DMA((1,))],
        limit=4,
        after=[o_near[-1]],
    )

    half = wide // 2
    given = swap(give, "narrow", 2, 1)
    (mark,) = call(join_kernel, "mark", [keep], [shaped(1, total, HEAD_DIM)], limit=1, hint=FILL)
    (head,) = call(pair_kernel, "pair", [keep, given], [shaped(total, HEAD_DIM, dtype=BF16)], limit=1, after=[mark])
    routes = [(2 * s + n, 2 * ((2 * s + n) % wide) + s // half) for s in range(wide) for n in range(2)]
    sent = head
    head = lax.ppermute(head, ("wide", "narrow"), routes)
    unit = out_cols * STEP // 32
    spans = [(lo, min(lo + unit, o_cuts[2])) for lo in range(o_cuts[1], o_cuts[2], unit)]
    q, *pieces = call(
        functools.partial(query_kernel, spans=spans),
        "query",
        [x, near(w_query)] + [w_out] * len(spans),
        [shaped(total, q_cols)] + [fetched(w_out, *span) for span in spans],
        [pltpu.SemaphoreType.DMA((len(spans),))],
        limit=2,
        far=len(spans),
        after=[sent],
    )
    o_near += pieces
    (q,) = call(pack_kernel, "pack", [head, q], [shaped(total, HEAD_DIM + q_cols)], limit=1)
    other = swap(q, "narrow", 2, 1)
    (w,) = ahead("ahead", [w_out], [(o_cuts[2], o_cuts[3])], after=[q])
    o_near.append(w)

    def output(name, head, weights, own, spans):
        own_cols = [hi - lo for lo, hi in own]
        width = sum(w.shape[1] for w in weights) + sum(own_cols)
        return call(
            functools.partial(output_kernel, first=len(head) > 1, parts=len(weights), own=own, spans=spans),
            name,
            [*head, *[near(w) for w in weights], *([w_out] if own or spans else [])],
            ([shaped(total, q_cols, dtype=BF16)] if len(head) > 1 else [])
            + [shaped(wide // 2, rows, width), shaped(wide // 2, rows, width, dtype=BF16)]
            + [fetched(w_out, *span) for span in spans],
            [pltpu.VMEM((total, width), F32), pltpu.SemaphoreType.DMA((max(1, len(own) + len(spans)),))]
            + [pltpu.VMEM((w_out.shape[0], cols), BF16) for cols in own_cols],
            limit=8,
            far=1 if own or spans else 0,
        )

    att, keep0, send0, o2 = output(
        "output0",
        [q, other, turn, allow],
        o_near,
        [(o_cuts[3], o_cuts[4])],
        [(o_cuts[4], o_cuts[5])],
    )
    got0 = swap(send0, "wide", wide, 1)
    keep1, send1 = output("output1", [att], [o2], [], [])
    got1 = swap(send1, "wide", wide, 1)
    mine, *others = call(
        functools.partial(near_sum_kernel, parts=2),
        "pairs",
        [keep0, got0, keep1, got1],
        [shaped(rows, out_cols)] + [shaped(rows, out_cols, dtype=BF16)] * (half - 1),
        limit=1,
    )
    back = {k: swap(others[k - 1], "wide", wide, 2 * k) for k in reversed(range(1, half))}
    return call(total_kernel, "total", [mine] + [back[k] for k in reversed(range(1, half))], [shaped(rows, out_cols, dtype=BF16)], limit=1)[0]


def solution(mesh):
    in_specs = (
        P(("groups", "wide"), "narrow"),
        P("groups"),
        P("narrow", "wide"),
        P("narrow", "wide"),
        P("wide", "narrow"),
    )
    out_specs = P(("groups", "wide"), "narrow")
    body = local if mesh.shape["wide"] == KV_HEADS and mesh.shape["narrow"] == 2 else plain
    return jax.shard_map(body, mesh=mesh, in_specs=in_specs, out_specs=out_specs, check_vma=False)
```

```python
import functools
import math

import jax
import jax.numpy as jnp
from jax import lax
from jax.experimental import pallas as pl
from jax.experimental.pallas import tpu as pltpu
from jax.sharding import PartitionSpec as P

HEADS = 128
KV_HEADS = 8
HEAD_DIM = 128
theta_base = 500000.0
F32 = jnp.float32
BF16 = jnp.bfloat16
MIB = 1 << 20
CUTS = (0, 4, 16, 18, 24, 30, 32)
STEP = 4
FILL = 9 * 10**9


def vspec():
    return pl.BlockSpec(memory_space=pltpu.VMEM)


def aspec():
    return pl.BlockSpec(memory_space=pltpu.HBM)


def near(x):
    return pltpu.with_memory_space_constraint(x, pltpu.VMEM)


def call(kernel, name, ins, outs, scratch=(), limit=4, far=0, hint=0, smem=0, after=(), behind=()):
    if after:
        inner, skip = kernel, len(after)
        kernel = lambda *refs: inner(*refs[skip:])
        ins = [*[near(x) for x in after], *ins]
    if behind:
        whole, drop, keep = kernel, len(behind), len(ins) + len(after)
        kernel = lambda *refs: whole(*refs[:keep], *refs[keep + drop :])
        ins, far = [*ins, *behind], far + drop
    if far:
        ins = [*ins[:-far], *[pltpu.with_memory_space_constraint(x, pltpu.HBM) for x in ins[-far:]]]
    specs = [pl.BlockSpec(memory_space=pltpu.SMEM)] * smem
    specs += [vspec()] * (len(ins) - smem - far) + [aspec()] * far
    return pl.pallas_call(
        kernel,
        out_shape=tuple(outs),
        in_specs=specs,
        out_specs=(vspec(),) * len(outs),
        scratch_shapes=list(scratch),
        compiler_params=pltpu.CompilerParams(vmem_limit_bytes=limit * MIB),
        cost_estimate=pl.CostEstimate(flops=hint, bytes_accessed=1000, transcendentals=0),
        name=name,
    )(*ins)


def fetched(w, lo, hi):
    return pltpu.VMEM((w.shape[0], hi - lo), BF16)


def fetches(sources, targets, spans, sems):
    return [
        pltpu.make_async_copy(src.at[:, pl.ds(lo, hi - lo)], dst, sems.at[i])
        for i, (src, dst, (lo, hi)) in enumerate(zip(sources, targets, spans))
    ]


def ahead_kernel(*refs, spans):
    n = len(spans)
    copies = fetches(refs[:n], refs[n : 2 * n], spans, refs[-1])
    for copy in copies:
        copy.start()
    for copy in copies:
        copy.wait()


def ahead(name, sources, spans, after=(), behind=(), hint=0):
    return call(
        functools.partial(ahead_kernel, spans=spans),
        name,
        sources,
        [fetched(w, lo, hi) for w, (lo, hi) in zip(sources, spans)],
        [pltpu.SemaphoreType.DMA((len(spans),))],
        limit=1,
        far=len(sources),
        hint=hint,
        after=after,
        behind=behind,
    )


def positions(token, len_ref):
    end = jnp.int32(0)
    segment = jnp.zeros_like(token)
    start = jnp.zeros_like(token)
    for i in range(len_ref.shape[0]):
        end = end + len_ref[i]
        past = token >= end
        segment = segment + past.astype(jnp.int32)
        start = start + jnp.where(past, len_ref[i], 0)
    return segment, token - start


def tables_kernel(*refs, rows, spans):
    n = len(spans)
    sources, (turn_ref, allow_ref), targets, (sems, len_ref, len_sem) = refs[: n + 1], refs[n + 1 : n + 3], refs[n + 3 : -3], refs[-3:]
    lengths = pltpu.make_async_copy(sources[0], len_ref, len_sem)
    lengths.start()
    copies = fetches(sources[1:], targets, spans, sems)
    for copy in copies:
        copy.start()
    me = lax.axis_index("wide")
    total, dim = turn_ref.shape[1:]

    def owner(row, base):
        return rows * jnp.bitwise_xor(row // rows, base) + lax.rem(row, rows)

    shape = (total, dim)
    power = lax.rem(lax.broadcasted_iota(jnp.int32, shape, 1), dim // 2).astype(F32)
    freq = jnp.exp(power * F32(-2.0 * math.log(theta_base) / dim))
    lengths.wait()
    row = lax.broadcasted_iota(jnp.int32, shape, 0)
    lane = lax.broadcasted_iota(jnp.int32, shape, 1)
    for i, base in enumerate((me, me // 2)):
        angle = positions(owner(row, base), len_ref)[1].astype(F32) * freq
        sine = jnp.sin(angle)
        turn_ref[2 * i] = jnp.cos(angle)
        turn_ref[2 * i + 1] = jnp.where(lane < dim // 2, -sine, sine)
    shape = allow_ref.shape
    query = owner(lax.rem(lax.broadcasted_iota(jnp.int32, shape, 0), total), me)
    key = owner(lax.broadcasted_iota(jnp.int32, shape, 1), me // 2)
    same = positions(query, len_ref)[0] == positions(key, len_ref)[0]
    allow_ref[...] = jnp.where(same & (key <= query), 1.0, 0.0).astype(F32)
    for copy in copies:
        copy.wait()


def join_kernel(*refs):
    for i, ref in enumerate(refs[:-1]):
        refs[-1][i] = ref[...]


def keyval_kernel(*refs, order, spans):
    n = len(spans)
    parts, w_ref, refs = refs[: len(order)], refs[len(order)], refs[len(order) + 1 :]
    sources, (x_out, keep_ref, give_ref), targets = refs[:n], refs[n : n + 3], refs[n + 3 : 2 * n + 3]
    x32, sems = refs[2 * n + 3 :]
    copies = fetches(sources, targets, spans, sems)
    for copy in copies:
        copy.start()
    rows = parts[0].shape[1]
    for ref, owners in zip(parts, order):
        for i, s in enumerate(owners):
            x32[rows * s : rows * (s + 1), :] = ref[i].astype(F32)
    x_out[...] = x32[...].astype(BF16)
    part = jnp.dot(x_out[...], w_ref[...], preferred_element_type=F32)
    width = keep_ref.shape[1]
    left, right = part[:, :width], part[:, width:]
    low = lax.axis_index("narrow") == 0
    keep_ref[...] = jnp.where(low, left, right)
    give_ref[...] = jnp.where(low, right, left)
    for copy in copies:
        copy.wait()


def pair_kernel(mine_ref, other_ref, out_ref):
    out_ref[...] = (mine_ref[...] + other_ref[...]).astype(BF16)


def multiply(x_ref, w_ref, out, at, lo=0, hi=None):
    width = (w_ref.shape[1] if hi is None else hi) - lo
    step = math.gcd(math.gcd(width, min(1024, (1 << 23) // w_ref.shape[0])), lo)

    @pl.loop(0, width // step)
    def _(j):
        cols = pl.ds(pl.multiple_of(lo + j * step, step), step)
        part = jnp.dot(x_ref[...], w_ref[:, cols], preferred_element_type=F32)
        out[:, pl.ds(pl.multiple_of(at + j * step, step), step)] = part


def query_kernel(x_ref, w_ref, *refs, spans):
    n = len(spans)
    sources, q_out, targets, sems = refs[:n], refs[n], refs[n + 1 : -1], refs[-1]
    copies = fetches(sources, targets, spans, sems)
    for copy in copies:
        copy.start()
    multiply(x_ref, w_ref, q_out, 0)
    for copy in copies:
        copy.wait()


def pack_kernel(*refs):
    at = 0
    for ref in refs[:-1]:
        refs[-1][:, at : at + ref.shape[1]] = ref[...].astype(F32)
        at += ref.shape[1]


def attend(mine_ref, other_ref, turn_ref, allow_ref, att):
    total, dim = turn_ref.shape[1:]
    low = lax.axis_index("narrow") == 0
    mine, other = mine_ref[:, :dim], other_ref[:, :dim]
    keys, values = jnp.where(low, mine, other), jnp.where(low, other, mine)
    summed = mine_ref[:, dim:] + other_ref[:, dim:]
    values = jnp.concatenate([values[total // 2 :], values[: total // 2]], axis=0).astype(BF16)

    def rotate(u, i):
        return (u * turn_ref[i] + pltpu.roll(u, dim // 2, 1) * turn_ref[i + 1]).astype(BF16)

    keys = rotate(keys, 2)
    heads = summed.shape[1] // dim
    stack = jnp.concatenate([rotate(summed[:, dim * h : dim * (h + 1)], 0) for h in range(heads)], axis=0)
    scores = lax.dot_general(stack, keys, (((1,), (1,)), ((), ())), preferred_element_type=F32)
    scores = scores / F32(math.sqrt(dim))
    scores = jnp.where(allow_ref[...] > 0, scores, F32(-1e30))
    weights = jnp.exp(scores - jnp.max(scores, axis=1, keepdims=True))
    probs = (weights / jnp.sum(weights, axis=1, keepdims=True)).astype(BF16)
    mixed = jnp.dot(probs, values, preferred_element_type=F32).astype(BF16)
    for h in range(heads):
        att[:, dim * h : dim * (h + 1)] = mixed[total * h : total * (h + 1), :]


def part_out(acc, keep_ref, send_ref):
    pieces = 2 * keep_ref.shape[0]
    rows = acc.shape[0] // pieces
    for s in range(0, pieces, 2):
        keep_ref[s // 2] = acc[rows * s : rows * (s + 1), :]
        send_ref[s // 2] = acc[rows * (s + 1) : rows * (s + 2), :].astype(BF16)


def output_kernel(*refs, first, parts, own, spans):
    n = len(spans)
    if first:
        head, refs = refs[:4], refs[4:]
    else:
        att, refs = refs[0], refs[1:]
    w_refs, refs = refs[:parts], refs[parts:]
    w_far = None
    if n or own:
        w_far, refs = refs[0], refs[1:]
    if first:
        att, refs = refs[0], refs[1:]
    keep_ref, send_ref, targets, refs = refs[0], refs[1], refs[2 : 2 + n], refs[2 + n :]
    acc, sems, mine = refs[0], refs[1], refs[2:]
    copies = fetches([w_far] * (len(own) + n), [*mine, *targets], [*own, *spans], sems)
    for copy in copies:
        copy.start()
    if first:
        attend(*head, att)
    at = 0
    for w_ref in w_refs:
        multiply(att, w_ref, acc, at)
        at += w_ref.shape[1]
    for copy, w_ref in zip(copies, mine):
        copy.wait()
        multiply(att, w_ref, acc, at)
        at += w_ref.shape[1]
    part_out(acc, keep_ref, send_ref)
    for copy in copies[len(own) :]:
        copy.wait()


def near_sum_kernel(*refs, parts):
    at = 0
    outs = refs[2 * parts :]
    for p in range(parts):
        keep_ref, got_ref = refs[2 * p : 2 * p + 2]
        width = keep_ref.shape[2]
        for k in range(keep_ref.shape[0]):
            part = keep_ref[k] + got_ref[k].astype(F32)
            outs[k][:, at : at + width] = part.astype(outs[k].dtype)
        at += width


def total_kernel(*refs):
    total = refs[0][...]
    for r in refs[1:-1]:
        total = total + r[...].astype(F32)
    refs[-1][...] = total.astype(BF16)


def swap(x, axis, size, bit):
    return lax.ppermute(x, axis, [(i, i ^ bit) for i in range(size)])


def shaped(*shape, dtype=F32):
    return jax.ShapeDtypeStruct(shape, dtype)


def plain_positions(lengths, total):
    index = jnp.arange(total, dtype=jnp.int32)
    ends = jnp.cumsum(lengths)
    past = index[:, None] >= ends[None, :]
    segment = jnp.sum(past.astype(jnp.int32), axis=1)
    offset = index - jnp.sum(jnp.where(past, lengths[None, :], 0), axis=1)
    return segment, offset


def plain_rotate(values, offset):
    half = values.shape[-1] // 2
    freq = theta_base ** (-(jnp.arange(half, dtype=F32) * 2.0) / values.shape[-1])
    angle = offset.astype(F32)[:, None] * freq[None, :]
    cosine = jnp.cos(angle)[:, None, :]
    sine = jnp.sin(angle)[:, None, :]
    first, second = values[..., :half], values[..., half:]
    return jnp.concatenate([first * cosine - second * sine, second * cosine + first * sine], axis=-1)


def plain_attend(query, keys, values, segment):
    total = query.shape[0]
    scores = jnp.einsum("qhd,khd->hqk", query, keys, preferred_element_type=F32) / jnp.sqrt(F32(query.shape[-1]))
    index = jnp.arange(total, dtype=jnp.int32)
    allowed = (segment[:, None] == segment[None, :]) & (index[None, :] <= index[:, None])
    scores = jnp.where(allowed[None], scores, F32(-1e30))
    weights = jnp.exp(scores - jnp.max(scores, axis=-1, keepdims=True))
    probs = (weights / jnp.sum(weights, axis=-1, keepdims=True)).astype(BF16)
    return jnp.einsum("hqk,khd->qhd", probs, values, preferred_element_type=F32).astype(BF16)


def plain(tokens, lengths, w_query, w_keyval, w_out):
    q_cols = w_query.shape[1]
    heads = q_cols // HEAD_DIM
    piece = lax.all_gather(tokens, "wide", axis=0, tiled=True)
    query_part = jnp.dot(piece, w_query, preferred_element_type=F32)
    keyval_part = jnp.dot(piece, w_keyval, preferred_element_type=F32)
    total = piece.shape[0]
    query = lax.psum(query_part, "narrow")
    summed = lax.psum(keyval_part, "narrow").astype(BF16)
    keyval = lax.all_gather(summed, "wide", axis=1, tiled=True)
    segment, offset = plain_positions(lengths, total)
    kv_width = KV_HEADS * HEAD_DIM
    keys = plain_rotate(keyval[:, :kv_width].astype(F32).reshape(total, KV_HEADS, HEAD_DIM), offset).astype(BF16)
    values = keyval[:, kv_width:].reshape(total, KV_HEADS, HEAD_DIM)
    head_ids = lax.axis_index("wide") * heads + jnp.arange(heads, dtype=jnp.int32)
    kv_ids = head_ids // (HEADS // KV_HEADS)
    query_rot = plain_rotate(query.reshape(total, -1, HEAD_DIM), offset).astype(BF16)
    attended = plain_attend(query_rot, jnp.take(keys, kv_ids, axis=1), jnp.take(values, kv_ids, axis=1), segment)
    mixed = lax.psum_scatter(
        jnp.dot(attended.reshape(total, -1), w_out, preferred_element_type=F32), "wide", scatter_dimension=0, tiled=True
    )
    return mixed.astype(BF16)


def local(tokens, lengths, w_query, w_keyval, w_out):
    wide = lax.axis_size("wide")
    rows, depth = tokens.shape
    total = rows * wide
    kv_cols, q_cols, out_cols = w_keyval.shape[1], w_query.shape[1], w_out.shape[1]
    heads = q_cols // HEAD_DIM

    o_cuts = [out_cols * k // 32 for k in CUTS]
    o_near, spans = [], [(o_cuts[0], o_cuts[1])]
    along = list(reversed(range(2, wide, 2)))
    other = swap(tokens, "wide", wide, 1)
    turn, allow, w = call(
        functools.partial(tables_kernel, rows=rows, spans=spans),
        "tables",
        [lengths, w_out],
        [shaped(4, total, HEAD_DIM), shaped(heads * total, total)] + [fetched(w_out, *s) for s in spans],
        [pltpu.SemaphoreType.DMA((1,)), pltpu.SMEM(lengths.shape, jnp.int32), pltpu.SemaphoreType.DMA],
        limit=2,
        far=2,
    )
    o_near.append(w)
    (pair,) = call(join_kernel, "join", [tokens, other], [shaped(2, rows, depth, dtype=BF16)], limit=2, after=[turn])
    others = [swap(pair, "wide", wide, bit) for bit in along]
    others, along = others[::-1], along[::-1]
    order = [[bit, bit ^ 1] for bit in [*along, 0]]
    x, keep, give = call(
        functools.partial(keyval_kernel, order=order, spans=[]),
        "keyval",
        [*others, pair, near(w_keyval)],
        [shaped(total, depth, dtype=BF16)] + [shaped(total, HEAD_DIM)] * 2,
        [pltpu.VMEM((total, depth), F32), pltpu.SemaphoreType.DMA((1,))],
        limit=4,
        after=[o_near[-1]],
    )

    half = wide // 2
    given = swap(give, "narrow", 2, 1)
    (mark,) = call(join_kernel, "mark", [keep], [shaped(1, total, HEAD_DIM)], limit=1, hint=FILL)
    (head,) = call(pair_kernel, "pair", [keep, given], [shaped(total, HEAD_DIM, dtype=BF16)], limit=1, after=[mark])
    routes = [(2 * s + n, 2 * ((2 * s + n) % wide) + s // half) for s in range(wide) for n in range(2)]
    sent = head
    head = lax.ppermute(head, ("wide", "narrow"), routes)
    unit = out_cols * STEP // 32
    spans = [(lo, min(lo + unit, o_cuts[2])) for lo in range(o_cuts[1], o_cuts[2], unit)]
    q, *pieces = call(
        functools.partial(query_kernel, spans=spans),
        "query",
        [x, near(w_query)] + [w_out] * len(spans),
        [shaped(total, q_cols)] + [fetched(w_out, *span) for span in spans],
        [pltpu.SemaphoreType.DMA((len(spans),))],
        limit=2,
        far=len(spans),
        after=[sent],
    )
    o_near += pieces
    (q,) = call(pack_kernel, "pack", [head, q], [shaped(total, HEAD_DIM + q_cols)], limit=1)
    other = swap(q, "narrow", 2, 1)
    (w,) = ahead("ahead", [w_out], [(o_cuts[2], o_cuts[3])], after=[q])
    o_near.append(w)

    def output(name, head, weights, own, spans):
        own_cols = [hi - lo for lo, hi in own]
        width = sum(w.shape[1] for w in weights) + sum(own_cols)
        return call(
            functools.partial(output_kernel, first=len(head) > 1, parts=len(weights), own=own, spans=spans),
            name,
            [*head, *[near(w) for w in weights], *([w_out] if own or spans else [])],
            ([shaped(total, q_cols, dtype=BF16)] if len(head) > 1 else [])
            + [shaped(wide // 2, rows, width), shaped(wide // 2, rows, width, dtype=BF16)]
            + [fetched(w_out, *span) for span in spans],
            [pltpu.VMEM((total, width), F32), pltpu.SemaphoreType.DMA((max(1, len(own) + len(spans)),))]
            + [pltpu.VMEM((w_out.shape[0], cols), BF16) for cols in own_cols],
            limit=8,
            far=1 if own or spans else 0,
        )

    att, keep0, send0, o2 = output(
        "output0",
        [q, other, turn, allow],
        o_near,
        [(o_cuts[3], o_cuts[4])],
        [(o_cuts[4], o_cuts[5])],
    )
    got0 = swap(send0, "wide", wide, 1)
    keep1, send1 = output("output1", [att], [o2], [(o_cuts[5], o_cuts[6])], [])
    got1 = swap(send1, "wide", wide, 1)
    mine, *others = call(
        functools.partial(near_sum_kernel, parts=2),
        "pairs",
        [keep0, got0, keep1, got1],
        [shaped(rows, out_cols)] + [shaped(rows, out_cols, dtype=BF16)] * (half - 1),
        limit=1,
    )
    back = {k: swap(others[k - 1], "wide", wide, 2 * k) for k in reversed(range(1, half))}
    return call(total_kernel, "total", [mine] + [back[k] for k in reversed(range(1, half))], [shaped(rows, out_cols, dtype=BF16)], limit=1)[0]


def solution(mesh):
    in_specs = (
        P(("groups", "wide"), "narrow"),
        P("groups"),
        P("narrow", "wide"),
        P("narrow", "wide"),
        P("wide", "narrow"),
    )
    out_specs = P(("groups", "wide"), "narrow")
    body = local if mesh.shape["wide"] == KV_HEADS and mesh.shape["narrow"] == 2 else plain
    return jax.shard_map(body, mesh=mesh, in_specs=in_specs, out_specs=out_specs, check_vma=False)
```

```python
import functools
import math

import jax
import jax.numpy as jnp
from jax import lax
from jax.experimental import pallas as pl
from jax.experimental.pallas import tpu as pltpu
from jax.sharding import PartitionSpec as P

HEADS = 128
KV_HEADS = 8
HEAD_DIM = 128
theta_base = 500000.0
F32 = jnp.float32
BF16 = jnp.bfloat16
MIB = 1 << 20
CUTS = (0, 4, 16, 18, 24, 30, 32)
STEP = 4
FILL = 9 * 10**9


def vspec():
    return pl.BlockSpec(memory_space=pltpu.VMEM)


def aspec():
    return pl.BlockSpec(memory_space=pltpu.HBM)


def near(x):
    return pltpu.with_memory_space_constraint(x, pltpu.VMEM)


def call(kernel, name, ins, outs, scratch=(), limit=4, far=0, hint=0, smem=0, after=(), behind=()):
    if after:
        inner, skip = kernel, len(after)
        kernel = lambda *refs: inner(*refs[skip:])
        ins = [*[near(x) for x in after], *ins]
    if behind:
        whole, drop, keep = kernel, len(behind), len(ins) + len(after)
        kernel = lambda *refs: whole(*refs[:keep], *refs[keep + drop :])
        ins, far = [*ins, *behind], far + drop
    if far:
        ins = [*ins[:-far], *[pltpu.with_memory_space_constraint(x, pltpu.HBM) for x in ins[-far:]]]
    specs = [pl.BlockSpec(memory_space=pltpu.SMEM)] * smem
    specs += [vspec()] * (len(ins) - smem - far) + [aspec()] * far
    return pl.pallas_call(
        kernel,
        out_shape=tuple(outs),
        in_specs=specs,
        out_specs=(vspec(),) * len(outs),
        scratch_shapes=list(scratch),
        compiler_params=pltpu.CompilerParams(vmem_limit_bytes=limit * MIB),
        cost_estimate=pl.CostEstimate(flops=hint, bytes_accessed=1000, transcendentals=0),
        name=name,
    )(*ins)


def fetched(w, lo, hi):
    return pltpu.VMEM((w.shape[0], hi - lo), BF16)


def fetches(sources, targets, spans, sems):
    return [
        pltpu.make_async_copy(src.at[:, pl.ds(lo, hi - lo)], dst, sems.at[i])
        for i, (src, dst, (lo, hi)) in enumerate(zip(sources, targets, spans))
    ]


def ahead_kernel(*refs, spans):
    n = len(spans)
    copies = fetches(refs[:n], refs[n : 2 * n], spans, refs[-1])
    for copy in copies:
        copy.start()
    for copy in copies:
        copy.wait()


def ahead(name, sources, spans, after=(), behind=(), hint=0):
    return call(
        functools.partial(ahead_kernel, spans=spans),
        name,
        sources,
        [fetched(w, lo, hi) for w, (lo, hi) in zip(sources, spans)],
        [pltpu.SemaphoreType.DMA((len(spans),))],
        limit=1,
        far=len(sources),
        hint=hint,
        after=after,
        behind=behind,
    )


def positions(token, len_ref):
    end = jnp.int32(0)
    segment = jnp.zeros_like(token)
    start = jnp.zeros_like(token)
    for i in range(len_ref.shape[0]):
        end = end + len_ref[i]
        past = token >= end
        segment = segment + past.astype(jnp.int32)
        start = start + jnp.where(past, len_ref[i], 0)
    return segment, token - start


def tables_kernel(*refs, rows, spans):
    n = len(spans)
    sources, (turn_ref, allow_ref), targets, (sems, len_ref, len_sem) = refs[: n + 1], refs[n + 1 : n + 3], refs[n + 3 : -3], refs[-3:]
    lengths = pltpu.make_async_copy(sources[0], len_ref, len_sem)
    lengths.start()
    copies = fetches(sources[1:], targets, spans, sems)
    for copy in copies:
        copy.start()
    me = lax.axis_index("wide")
    total, dim = turn_ref.shape[1:]

    def owner(row, base):
        return rows * jnp.bitwise_xor(row // rows, base) + lax.rem(row, rows)

    shape = (total, dim)
    power = lax.rem(lax.broadcasted_iota(jnp.int32, shape, 1), dim // 2).astype(F32)
    freq = jnp.exp(power * F32(-2.0 * math.log(theta_base) / dim))
    lengths.wait()
    row = lax.broadcasted_iota(jnp.int32, shape, 0)
    lane = lax.broadcasted_iota(jnp.int32, shape, 1)
    for i, base in enumerate((me, me // 2)):
        angle = positions(owner(row, base), len_ref)[1].astype(F32) * freq
        sine = jnp.sin(angle)
        turn_ref[2 * i] = jnp.cos(angle)
        turn_ref[2 * i + 1] = jnp.where(lane < dim // 2, -sine, sine)
    shape = allow_ref.shape
    query = owner(lax.rem(lax.broadcasted_iota(jnp.int32, shape, 1), total), me)
    key = owner(lax.broadcasted_iota(jnp.int32, shape, 0), me // 2)
    same = positions(query, len_ref)[0] == positions(key, len_ref)[0]
    allow_ref[...] = jnp.where(same & (key <= query), 1.0, 0.0).astype(F32)
    for copy in copies:
        copy.wait()


def join_kernel(*refs):
    for i, ref in enumerate(refs[:-1]):
        refs[-1][i] = ref[...]


def keyval_kernel(*refs, order, spans):
    n = len(spans)
    parts, w_ref, refs = refs[: len(order)], refs[len(order)], refs[len(order) + 1 :]
    sources, (x_out, keep_ref, give_ref), targets = refs[:n], refs[n : n + 3], refs[n + 3 : 2 * n + 3]
    x32, sems = refs[2 * n + 3 :]
    copies = fetches(sources, targets, spans, sems)
    for copy in copies:
        copy.start()
    rows = parts[0].shape[1]
    for ref, owners in zip(parts, order):
        for i, s in enumerate(owners):
            x32[rows * s : rows * (s + 1), :] = ref[i].astype(F32)
    x_out[...] = x32[...].astype(BF16)
    part = jnp.dot(x_out[...], w_ref[...], preferred_element_type=F32)
    width = keep_ref.shape[1]
    left, right = part[:, :width], part[:, width:]
    low = lax.axis_index("narrow") == 0
    keep_ref[...] = jnp.where(low, left, right)
    give_ref[...] = jnp.where(low, right, left)
    for copy in copies:
        copy.wait()


def pair_kernel(mine_ref, other_ref, out_ref):
    out_ref[...] = (mine_ref[...] + other_ref[...]).astype(BF16)


def multiply(x_ref, w_ref, out, at, lo=0, hi=None):
    width = (w_ref.shape[1] if hi is None else hi) - lo
    step = math.gcd(math.gcd(width, min(1024, (1 << 23) // w_ref.shape[0])), lo)

    @pl.loop(0, width // step)
    def _(j):
        cols = pl.ds(pl.multiple_of(lo + j * step, step), step)
        part = jnp.dot(x_ref[...], w_ref[:, cols], preferred_element_type=F32)
        out[:, pl.ds(pl.multiple_of(at + j * step, step), step)] = part


def query_kernel(x_ref, w_ref, *refs, spans):
    n = len(spans)
    sources, q_out, targets, sems = refs[:n], refs[n], refs[n + 1 : -1], refs[-1]
    copies = fetches(sources, targets, spans, sems)
    for copy in copies:
        copy.start()
    multiply(x_ref, w_ref, q_out, 0)
    for copy in copies:
        copy.wait()


def pack_kernel(*refs):
    at = 0
    for ref in refs[:-1]:
        refs[-1][:, at : at + ref.shape[1]] = ref[...].astype(F32)
        at += ref.shape[1]


def attend(mine_ref, other_ref, turn_ref, allow_ref, att):
    total, dim = turn_ref.shape[1:]
    low = lax.axis_index("narrow") == 0
    mine, other = mine_ref[:, :dim], other_ref[:, :dim]
    keys, values = jnp.where(low, mine, other), jnp.where(low, other, mine)
    summed = mine_ref[:, dim:] + other_ref[:, dim:]
    values = jnp.concatenate([values[total // 2 :], values[: total // 2]], axis=0).astype(BF16)

    def rotate(u, i):
        return (u * turn_ref[i] + pltpu.roll(u, dim // 2, 1) * turn_ref[i + 1]).astype(BF16)

    keys = rotate(keys, 2)
    heads = summed.shape[1] // dim
    stack = jnp.concatenate([rotate(summed[:, dim * h : dim * (h + 1)], 0) for h in range(heads)], axis=0)
    scores = lax.dot_general(keys, stack, (((1,), (1,)), ((), ())), preferred_element_type=F32)
    scores = scores / F32(math.sqrt(dim))
    scores = jnp.where(allow_ref[...] > 0, scores, F32(-1e30))
    weights = jnp.exp(scores - jnp.max(scores, axis=0, keepdims=True))
    probs = (weights / jnp.sum(weights, axis=0, keepdims=True)).astype(BF16)
    mixed = lax.dot_general(probs, values, (((0,), (0,)), ((), ())), preferred_element_type=F32).astype(BF16)
    for h in range(heads):
        att[:, dim * h : dim * (h + 1)] = mixed[total * h : total * (h + 1), :]


def part_out(acc, keep_ref, send_ref):
    pieces = 2 * keep_ref.shape[0]
    rows = acc.shape[0] // pieces
    for s in range(0, pieces, 2):
        keep_ref[s // 2] = acc[rows * s : rows * (s + 1), :]
        send_ref[s // 2] = acc[rows * (s + 1) : rows * (s + 2), :].astype(BF16)


def output_kernel(*refs, first, parts, own, spans):
    n = len(spans)
    if first:
        head, refs = refs[:4], refs[4:]
    else:
        att, refs = refs[0], refs[1:]
    w_refs, refs = refs[:parts], refs[parts:]
    w_far = None
    if n or own:
        w_far, refs = refs[0], refs[1:]
    if first:
        att, refs = refs[0], refs[1:]
    keep_ref, send_ref, targets, refs = refs[0], refs[1], refs[2 : 2 + n], refs[2 + n :]
    acc, sems, mine = refs[0], refs[1], refs[2:]
    copies = fetches([w_far] * (len(own) + n), [*mine, *targets], [*own, *spans], sems)
    for copy in copies:
        copy.start()
    if first:
        attend(*head, att)
    at = 0
    for w_ref in w_refs:
        multiply(att, w_ref, acc, at)
        at += w_ref.shape[1]
    for copy, w_ref in zip(copies, mine):
        copy.wait()
        multiply(att, w_ref, acc, at)
        at += w_ref.shape[1]
    part_out(acc, keep_ref, send_ref)
    for copy in copies[len(own) :]:
        copy.wait()


def near_sum_kernel(*refs, parts):
    at = 0
    outs = refs[2 * parts :]
    for p in range(parts):
        keep_ref, got_ref = refs[2 * p : 2 * p + 2]
        width = keep_ref.shape[2]
        for k in range(keep_ref.shape[0]):
            part = keep_ref[k] + got_ref[k].astype(F32)
            outs[k][:, at : at + width] = part.astype(outs[k].dtype)
        at += width


def total_kernel(*refs):
    total = refs[0][...]
    for r in refs[1:-1]:
        total = total + r[...].astype(F32)
    refs[-1][...] = total.astype(BF16)


def swap(x, axis, size, bit):
    return lax.ppermute(x, axis, [(i, i ^ bit) for i in range(size)])


def shaped(*shape, dtype=F32):
    return jax.ShapeDtypeStruct(shape, dtype)


def plain_positions(lengths, total):
    index = jnp.arange(total, dtype=jnp.int32)
    ends = jnp.cumsum(lengths)
    past = index[:, None] >= ends[None, :]
    segment = jnp.sum(past.astype(jnp.int32), axis=1)
    offset = index - jnp.sum(jnp.where(past, lengths[None, :], 0), axis=1)
    return segment, offset


def plain_rotate(values, offset):
    half = values.shape[-1] // 2
    freq = theta_base ** (-(jnp.arange(half, dtype=F32) * 2.0) / values.shape[-1])
    angle = offset.astype(F32)[:, None] * freq[None, :]
    cosine = jnp.cos(angle)[:, None, :]
    sine = jnp.sin(angle)[:, None, :]
    first, second = values[..., :half], values[..., half:]
    return jnp.concatenate([first * cosine - second * sine, second * cosine + first * sine], axis=-1)


def plain_attend(query, keys, values, segment):
    total = query.shape[0]
    scores = jnp.einsum("qhd,khd->hqk", query, keys, preferred_element_type=F32) / jnp.sqrt(F32(query.shape[-1]))
    index = jnp.arange(total, dtype=jnp.int32)
    allowed = (segment[:, None] == segment[None, :]) & (index[None, :] <= index[:, None])
    scores = jnp.where(allowed[None], scores, F32(-1e30))
    weights = jnp.exp(scores - jnp.max(scores, axis=-1, keepdims=True))
    probs = (weights / jnp.sum(weights, axis=-1, keepdims=True)).astype(BF16)
    return jnp.einsum("hqk,khd->qhd", probs, values, preferred_element_type=F32).astype(BF16)


def plain(tokens, lengths, w_query, w_keyval, w_out):
    q_cols = w_query.shape[1]
    heads = q_cols // HEAD_DIM
    piece = lax.all_gather(tokens, "wide", axis=0, tiled=True)
    query_part = jnp.dot(piece, w_query, preferred_element_type=F32)
    keyval_part = jnp.dot(piece, w_keyval, preferred_element_type=F32)
    total = piece.shape[0]
    query = lax.psum(query_part, "narrow")
    summed = lax.psum(keyval_part, "narrow").astype(BF16)
    keyval = lax.all_gather(summed, "wide", axis=1, tiled=True)
    segment, offset = plain_positions(lengths, total)
    kv_width = KV_HEADS * HEAD_DIM
    keys = plain_rotate(keyval[:, :kv_width].astype(F32).reshape(total, KV_HEADS, HEAD_DIM), offset).astype(BF16)
    values = keyval[:, kv_width:].reshape(total, KV_HEADS, HEAD_DIM)
    head_ids = lax.axis_index("wide") * heads + jnp.arange(heads, dtype=jnp.int32)
    kv_ids = head_ids // (HEADS // KV_HEADS)
    query_rot = plain_rotate(query.reshape(total, -1, HEAD_DIM), offset).astype(BF16)
    attended = plain_attend(query_rot, jnp.take(keys, kv_ids, axis=1), jnp.take(values, kv_ids, axis=1), segment)
    mixed = lax.psum_scatter(
        jnp.dot(attended.reshape(total, -1), w_out, preferred_element_type=F32), "wide", scatter_dimension=0, tiled=True
    )
    return mixed.astype(BF16)


def local(tokens, lengths, w_query, w_keyval, w_out):
    wide = lax.axis_size("wide")
    rows, depth = tokens.shape
    total = rows * wide
    kv_cols, q_cols, out_cols = w_keyval.shape[1], w_query.shape[1], w_out.shape[1]
    heads = q_cols // HEAD_DIM

    o_cuts = [out_cols * k // 32 for k in CUTS]
    o_near, spans = [], [(o_cuts[0], o_cuts[1])]
    along = list(reversed(range(2, wide, 2)))
    other = swap(tokens, "wide", wide, 1)
    turn, allow, w = call(
        functools.partial(tables_kernel, rows=rows, spans=spans),
        "tables",
        [lengths, w_out],
        [shaped(4, total, HEAD_DIM), shaped(total, heads * total)] + [fetched(w_out, *s) for s in spans],
        [pltpu.SemaphoreType.DMA((1,)), pltpu.SMEM(lengths.shape, jnp.int32), pltpu.SemaphoreType.DMA],
        limit=2,
        far=2,
    )
    o_near.append(w)
    (pair,) = call(join_kernel, "join", [tokens, other], [shaped(2, rows, depth, dtype=BF16)], limit=2, after=[turn])
    others = [swap(pair, "wide", wide, bit) for bit in along]
    others, along = others[::-1], along[::-1]
    order = [[bit, bit ^ 1] for bit in [*along, 0]]
    x, keep, give = call(
        functools.partial(keyval_kernel, order=order, spans=[]),
        "keyval",
        [*others, pair, near(w_keyval)],
        [shaped(total, depth, dtype=BF16)] + [shaped(total, HEAD_DIM)] * 2,
        [pltpu.VMEM((total, depth), F32), pltpu.SemaphoreType.DMA((1,))],
        limit=4,
        after=[o_near[-1]],
    )

    half = wide // 2
    given = swap(give, "narrow", 2, 1)
    (mark,) = call(join_kernel, "mark", [keep], [shaped(1, total, HEAD_DIM)], limit=1, hint=FILL)
    (head,) = call(pair_kernel, "pair", [keep, given], [shaped(total, HEAD_DIM, dtype=BF16)], limit=1, after=[mark])
    routes = [(2 * s + n, 2 * ((2 * s + n) % wide) + s // half) for s in range(wide) for n in range(2)]
    sent = head
    head = lax.ppermute(head, ("wide", "narrow"), routes)
    unit = out_cols * STEP // 32
    spans = [(lo, min(lo + unit, o_cuts[2])) for lo in range(o_cuts[1], o_cuts[2], unit)]
    q, *pieces = call(
        functools.partial(query_kernel, spans=spans),
        "query",
        [x, near(w_query)] + [w_out] * len(spans),
        [shaped(total, q_cols)] + [fetched(w_out, *span) for span in spans],
        [pltpu.SemaphoreType.DMA((len(spans),))],
        limit=2,
        far=len(spans),
        after=[sent],
    )
    o_near += pieces
    (q,) = call(pack_kernel, "pack", [head, q], [shaped(total, HEAD_DIM + q_cols)], limit=1)
    other = swap(q, "narrow", 2, 1)
    (w,) = ahead("ahead", [w_out], [(o_cuts[2], o_cuts[3])], after=[q])
    o_near.append(w)

    def output(name, head, weights, own, spans):
        own_cols = [hi - lo for lo, hi in own]
        width = sum(w.shape[1] for w in weights) + sum(own_cols)
        return call(
            functools.partial(output_kernel, first=len(head) > 1, parts=len(weights), own=own, spans=spans),
            name,
            [*head, *[near(w) for w in weights], *([w_out] if own or spans else [])],
            ([shaped(total, q_cols, dtype=BF16)] if len(head) > 1 else [])
            + [shaped(wide // 2, rows, width), shaped(wide // 2, rows, width, dtype=BF16)]
            + [fetched(w_out, *span) for span in spans],
            [pltpu.VMEM((total, width), F32), pltpu.SemaphoreType.DMA((max(1, len(own) + len(spans)),))]
            + [pltpu.VMEM((w_out.shape[0], cols), BF16) for cols in own_cols],
            limit=8,
            far=1 if own or spans else 0,
        )

    att, keep0, send0, o2 = output(
        "output0",
        [q, other, turn, allow],
        o_near,
        [(o_cuts[3], o_cuts[4])],
        [(o_cuts[4], o_cuts[5])],
    )
    got0 = swap(send0, "wide", wide, 1)
    keep1, send1 = output("output1", [att], [o2], [(o_cuts[5], o_cuts[6])], [])
    got1 = swap(send1, "wide", wide, 1)
    mine, *others = call(
        functools.partial(near_sum_kernel, parts=2),
        "pairs",
        [keep0, got0, keep1, got1],
        [shaped(rows, out_cols)] + [shaped(rows, out_cols, dtype=BF16)] * (half - 1),
        limit=1,
    )
    back = {k: swap(others[k - 1], "wide", wide, 2 * k) for k in reversed(range(1, half))}
    return call(total_kernel, "total", [mine] + [back[k] for k in reversed(range(1, half))], [shaped(rows, out_cols, dtype=BF16)], limit=1)[0]


def solution(mesh):
    in_specs = (
        P(("groups", "wide"), "narrow"),
        P("groups"),
        P("narrow", "wide"),
        P("narrow", "wide"),
        P("wide", "narrow"),
    )
    out_specs = P(("groups", "wide"), "narrow")
    body = local if mesh.shape["wide"] == KV_HEADS and mesh.shape["narrow"] == 2 else plain
    return jax.shard_map(body, mesh=mesh, in_specs=in_specs, out_specs=out_specs, check_vma=False)
```
